512 devices in a mesh: ctx: 16 (over z_lo, y), head: 8 (over x, core), batch: 4 (over z_hi).
Axes of the slice: x: 4, y: 8, z: 8 (z_hi: 4, z_lo: 2; z = z_hi * 2 + z_lo), core: 2. Of those that a mesh axis runs over, the one named last changes fastest.
Arguments:
- ingest: bfloat16 [16, 4, 12, 128, 4, 1024], P('ctx', 'batch', None, None, None, 'head'), may hold values from -6 to 6
- src_shard: int32 [16, 4, 6], P('ctx'), may hold values from 0 to 3, as said below
- src_slot: int32 [16, 4, 6], P('ctx'), may hold values from 0 to 11
- hist_len: int32 [4, 4], P('batch'), may hold values from 1 to 6144, 12288 in all within a row
- w_out: bfloat16 [1024, 1024], P('head'), may hold values from -0.1875 to 0.1875
Outputs:
- mixed: bfloat16 [4, 12288, 1024], P('batch', 'ctx', 'head')
The draws below stay inside these ranges and needn't reach their ends.
Inputs may be any that keep to these rules, and one draw needn't show every extreme that they name: `src_shard`: for each owner index, every owner's 6 blocks come from exactly two different ingestion shards, 3 from each; no (shard, slot) pair of one owner index feeds two blocks. `hist_len`: the 4 histories of a group fill its 12288 positions in order.
All inputs are finite; a program needn't handle non-finite values.
Results may differ from the reference program's by a relative error of at most 0.0058.
Values may be sent and summed in bfloat16 or wider, within the bound.
No kernel may reach another device: no remote copies, remote signals or barrier semaphores. Data moves between devices by JAX's collectives and lax.ppermute only.
A program may use at most 64 MiB of HBM per device.

```python
import math
import jax
import jax.numpy as jnp
import numpy as np
from jax import lax

HD = 128
HEADS = 8
D = 1024
BLOCK = 128
BLK_DEV = 6
CAP = 3
GROUPS = 4
CTXS = 16
SLOTS = 12
ROWS_DEV = 768
SEQ = 12288
USERS = 4
HIST_MOST = 6144


def plan_blocks(key):

    def one_ctx(ctx_key):
        key_sources, key_slots, key_order = jax.random.split(ctx_key, 3)
        source_order = jax.vmap(lambda one_key: jax.random.permutation(one_key, GROUPS))(jax.random.split(key_sources, GROUPS))
        sources = source_order[:, :2].astype(jnp.int32)
        requests = sources.reshape(-1)
        request_pos = jnp.arange(2 * GROUPS)
        earlier = (requests[None, :] == requests[:, None]) & (request_pos[None, :] < request_pos[:, None])
        request_rank = jnp.sum(earlier.astype(jnp.int32), axis=1)
        slot_orders = jax.vmap(lambda one_key: jax.random.permutation(one_key, SLOTS))(jax.random.split(key_slots, GROUPS))
        wanted = request_rank[:, None] * CAP + jnp.arange(CAP, dtype=jnp.int32)[None, :]
        chosen_slots = jnp.take_along_axis(slot_orders[requests], wanted, axis=1)
        owner_slots = chosen_slots.reshape(GROUPS, BLK_DEV).astype(jnp.int32)
        owner_shards = jnp.repeat(sources, CAP, axis=1)
        block_order = jax.vmap(lambda one_key: jax.random.permutation(one_key, BLK_DEV))(jax.random.split(key_order, GROUPS))
        return (jnp.take_along_axis(owner_shards, block_order, axis=1), jnp.take_along_axis(owner_slots, block_order, axis=1))
    return jax.vmap(one_ctx)(jax.random.split(jax.random.fold_in(key, 7), CTXS))


def draw_src_shard(key, part):
    return plan_blocks(key)[0].astype(jnp.int32)


def draw_src_slot(key, part):
    return plan_blocks(key)[1].astype(jnp.int32)


def block_scale(own_key, shape, cuts, least, largest):
    def one(axis_at, blocks):
        heights = jax.random.uniform(jax.random.fold_in(jax.random.fold_in(own_key, 6), axis_at), (blocks,), jnp.float32, least / len(cuts), largest / len(cuts))
        return jnp.repeat(jnp.exp(heights), shape[axis_at] // blocks).reshape((-1,) + (1,) * (len(shape) - axis_at - 1))

    gain = one(*cuts[0])
    for cut in cuts[1:]:
        gain = gain * one(*cut)
    return gain


def profile(count, total, most, lean):
    loads = [(1 << 20) // math.isqrt(rank ** lean) + 1 for rank in range(2, count + 1)]
    spare, holding = total - most - (count - 1), [1] * (count - 1)
    while spare > 0:
        free = [i for i in range(count - 1) if holding[i] < most]
        mass, remaining = sum([loads[i] for i in free]), spare
        for i in free:
            addition = min(most - holding[i], max(1, remaining * loads[i] // mass), spare)
            holding[i] = holding[i] + addition
            spare = spare - addition
    return np.array([most] + holding)


def ragged(key, amount, total, most, slope):
    if amount == 2:
        one = jax.random.randint(key, (), max(1, total - most), min(most, total - 1) + 1)
        return jnp.stack([one, total - one])
    sizes = jnp.asarray(profile(amount, total, most, slope), jnp.int32)
    twos = (amount - 1) // 2
    source_of, receiver = sizes[1:1 + 2 * twos:2], sizes[2:2 + 2 * twos:2]
    room = jnp.minimum(source_of - 1, most - receiver)
    shifted = jax.random.randint(jax.random.fold_in(key, 1), (twos,), 0, 1 << 20) % (room + 1)
    sizes = sizes.at[1:1 + 2 * twos:2].set(source_of - shifted).at[2:2 + 2 * twos:2].set(receiver + shifted)
    return sizes[jax.random.permutation(jax.random.fold_in(key, 2), amount)]


def centred(own_key, shape, spread, reach, cuts=(), held_as=jnp.bfloat16):
    loudness = block_scale(own_key, shape, cuts, -0.22, 0.18) if cuts else 1.0
    array = jax.random.normal(own_key, shape, jnp.float32) * spread * loudness
    return jnp.minimum(jnp.maximum(array, -reach), reach).astype(held_as)


def setup_inputs(seed: int = 0) -> dict:
    keys = jax.random.split(jax.random.key(seed), 6)
    return {
        "ingest": centred(keys[0], (CTXS, GROUPS, SLOTS, BLOCK, 4, D), 1.0, 6.0, ((0, 16), (1, 4), (5, 8))),
        "src_shard": draw_src_shard(jax.random.fold_in(keys[5], 71), 0),
        "src_slot": draw_src_slot(jax.random.fold_in(keys[5], 71), 0),
        "hist_len": jax.vmap(lambda own: ragged(own, USERS, SEQ, HIST_MOST, 2))(jax.random.split(keys[3], GROUPS)).reshape((GROUPS, USERS)).astype(jnp.int32),
        "w_out": centred(keys[4], (D, D), D ** -0.5, 0.1875, ((0, 8),)),
    }


def reference(ingest, src_shard, src_slot, hist_len, w_out):
    ctx_ids = jnp.arange(CTXS, dtype=jnp.int32)[:, None, None]
    owned = ingest[ctx_ids, src_shard, src_slot]
    owned = jnp.transpose(owned, (1, 0, 2, 3, 4, 5)).reshape(GROUPS, SEQ, 4, HEADS, HD)
    score_scale = 1.0 / math.sqrt(HD)

    def per_group(group_args):
        group_rows, lengths = group_args
        seg_ends = jnp.cumsum(lengths).astype(jnp.int32)
        all_pos = jnp.arange(SEQ, dtype=jnp.int32)
        segment = lax.optimization_barrier(jnp.sum((all_pos[:, None] >= seg_ends[None, :]).astype(jnp.int32), axis=1))
        key_rows = group_rows[:, 1].astype(jnp.float32)
        value_rows = group_rows[:, 2].astype(jnp.float32)

        def per_block(offset):
            query_rows = lax.dynamic_slice_in_dim(group_rows, offset, ROWS_DEV, 0)
            query_pos = offset + jnp.arange(ROWS_DEV, dtype=jnp.int32)
            query_seg = lax.dynamic_slice_in_dim(segment, offset, ROWS_DEV, 0)
            scores = jnp.einsum('qhd,khd->hqk', query_rows[:, 0].astype(jnp.float32), key_rows) * score_scale
            visible = (query_seg[:, None] == segment[None, :]) & (all_pos[None, :] <= query_pos[:, None])
            weights = jnp.where(visible[None], jax.nn.silu(scores), 0.0).astype(jnp.bfloat16)
            weights = lax.optimization_barrier(weights).astype(jnp.float32)
            attended = jnp.einsum('hqk,khd->qhd', weights, value_rows)
            mean_square = lax.optimization_barrier(jnp.mean(attended * attended, axis=-1, keepdims=True))
            normed = attended * lax.rsqrt(mean_square + 1e-06)
            gated = (normed * query_rows[:, 3].astype(jnp.float32)).astype(jnp.bfloat16).reshape(ROWS_DEV, D)
            return jnp.dot(gated, w_out, preferred_element_type=jnp.float32).astype(jnp.bfloat16)
        offsets = jnp.arange(CTXS, dtype=jnp.int32) * ROWS_DEV
        return lax.map(per_block, offsets).reshape(SEQ, D)
    return lax.map(per_group, (owned, hist_len))
```

```python
import functools
import math

import jax
import jax.numpy as jnp
from jax import lax
from jax.experimental import pallas as pl
from jax.experimental.pallas import tpu as pltpu
from jax.sharding import PartitionSpec as P

HD = 128
BLOCK = 128
PER_OWNER = 6
CAPACITY = 3
GROUPS = 4
CTXS = 16
PLANE = 8
HEADS = 8
ROWS = BLOCK * PER_OWNER
CHUNK = ROWS // HEADS
TILE = 256
HALF_SCALE = 0.5 / math.sqrt(HD)
VMEM = pl.BlockSpec(memory_space=pltpu.VMEM)
SMEM = pl.BlockSpec(memory_space=pltpu.SMEM)
ANY = pl.BlockSpec(memory_space=pl.ANY)


def params():
    return pltpu.CompilerParams(vmem_limit_bytes=48 * 1024 * 1024)


def pick_kernel(kinds, shard_ref, slot_ref, ingest_ref, out_ref, buf, sems):
    me = lax.axis_index("batch")
    copies = []
    for g in range(GROUPS):
        seen = jnp.int32(0)
        slots = [jnp.int32(0)] * CAPACITY
        for k in range(PER_OWNER):
            hit = shard_ref[g, k] == me
            slot = slot_ref[g, k]
            for r in range(CAPACITY):
                slots[r] = jnp.where(hit & (seen == r), slot, slots[r])
            seen = seen + hit.astype(jnp.int32)
        for r in range(CAPACITY):
            at = g * CAPACITY + r
            copy = pltpu.make_async_copy(ingest_ref.at[slots[r]], buf.at[at], sems.at[at])
            copy.start()
            copies.append(copy)
    for at, copy in enumerate(copies):
        copy.wait()
        for place, kind in enumerate(kinds):
            out_ref[at, :, place * HD : (place + 1) * HD] = buf[at, :, kind, :]


def pick(shards, slots, ingested, kinds):
    count = GROUPS * CAPACITY
    return pl.pallas_call(
        functools.partial(pick_kernel, kinds),
        out_shape=jax.ShapeDtypeStruct((count, BLOCK, 2 * HD), jnp.bfloat16),
        in_specs=[SMEM, SMEM, ANY],
        out_specs=VMEM,
        scratch_shapes=[
            pltpu.VMEM((count, BLOCK, 4, HD), jnp.bfloat16),
            pltpu.SemaphoreType.DMA((count,)),
        ],
        compiler_params=params(),
    )(shards, slots, ingested)


def order_kernel(split, shard_ref, in_ref, *out_refs):
    me = lax.axis_index("batch")
    shards = [shard_ref[me, k] for k in range(PER_OWNER)]
    for k in range(PER_OWNER):
        rank = jnp.int32(0)
        for earlier in range(k):
            rank = rank + (shards[earlier] == shards[k]).astype(jnp.int32)
        block = in_ref[shards[k] * CAPACITY + rank]
        rows = slice(k * BLOCK, (k + 1) * BLOCK)
        if split:
            out_refs[0][rows, :] = block[:, :HD]
            out_refs[1][rows, :] = block[:, HD:]
        else:
            out_refs[0][rows, :] = block


def in_order(shards, blocks, split):
    width = HD if split else 2 * HD
    shape = jax.ShapeDtypeStruct((ROWS, width), jnp.bfloat16)
    return pl.pallas_call(
        functools.partial(order_kernel, split),
        out_shape=[shape] * (2 if split else 1),
        in_specs=[SMEM, VMEM],
        out_specs=[VMEM] * (2 if split else 1),
        compiler_params=params(),
    )(shards, blocks)


def unit_owner(me, kind, step):
    if kind == "up":
        return me - step
    plane, row = me // PLANE, me % PLANE
    return plane * PLANE + (row + step) % PLANE


def history_ends(hist_ref):
    ends, total = [], jnp.int32(0)
    for u in range(4):
        total = total + hist_ref[0, u]
        ends.append(total)
    return ends


def start_of(ends, pos):
    start = jnp.zeros_like(pos)
    for e in ends:
        start = jnp.where(pos >= e, jnp.maximum(start, e), start)
    return start


def silu_of_dot(q, k):
    s = lax.dot_general(q, k, (((1,), (1,)), ((), ())), preferred_element_type=jnp.float32)
    h = s * HALF_SCALE
    return h + h * jnp.tanh(h)


def add_units(ends, q_base, q_ref, units, acc_ref):
    def row_tile(t, _):
        rows = pl.ds(pl.multiple_of(t * TILE, TILE), TILE)
        first = q_base + t * TILE
        last = first + TILE - 1
        low, high = start_of(ends, first), start_of(ends, last)
        for owner, unit in units:
            base = owner * ROWS
            some = (base <= last) & (base + ROWS - 1 >= low)
            whole = (base + ROWS - 1 <= first) & (base >= high)

            @pl.when(whole)
            def _():
                w = silu_of_dot(q_ref[rows, :], unit[:, :HD]).astype(jnp.bfloat16)
                acc_ref[rows, :] += jnp.dot(w, unit[:, HD:], preferred_element_type=jnp.float32)

            @pl.when(some & jnp.logical_not(whole))
            def _():
                for part in range(ROWS // TILE):
                    k_first = base + part * TILE
                    keys = slice(part * TILE, (part + 1) * TILE)

                    @pl.when((k_first <= last) & (k_first + TILE - 1 >= low))
                    def _():
                        pos = first + lax.broadcasted_iota(jnp.int32, (TILE, TILE), 0)
                        key = k_first + lax.broadcasted_iota(jnp.int32, (TILE, TILE), 1)
                        seen = (key <= pos) & (key >= start_of(ends, pos))
                        w = silu_of_dot(q_ref[rows, :], unit[keys, :HD])
                        w = jnp.where(seen, w, 0.0).astype(jnp.bfloat16)
                        acc_ref[rows, :] += jnp.dot(
                            w, unit[keys, HD:], preferred_element_type=jnp.float32
                        )

        return 0

    lax.fori_loop(0, ROWS // TILE, row_tile, 0)


def attend_kernel(names, first, hist_ref, q_ref, *refs):
    units, refs = refs[: len(names)], refs[len(names) :]
    acc_ref = refs[-1]
    if first:
        acc_ref[...] = jnp.zeros_like(acc_ref)
    else:
        acc_ref[...] = refs[0][...]
    me = lax.axis_index("ctx")
    ends = history_ends(hist_ref)
    owners = [unit_owner(me, *name) for name in names]
    add_units(ends, me * ROWS, q_ref, list(zip(owners, units)), acc_ref)


def estimate(units):
    return pl.CostEstimate(
        flops=4 * ROWS * ROWS * HD * units, bytes_accessed=1 << 20, transcendentals=ROWS * ROWS * units
    )


def attend(hist, q, units, names, acc=None):
    first = acc is None
    return pl.pallas_call(
        functools.partial(attend_kernel, names, first),
        out_shape=jax.ShapeDtypeStruct((ROWS, HD), jnp.float32),
        in_specs=[SMEM] + [VMEM] * (1 + len(units) + (0 if first else 1)),
        out_specs=VMEM,
        cost_estimate=estimate(len(units)),
        compiler_params=params(),
    )(hist, q, *units, *(() if first else (acc,)))


def lent_kernel(names, hist_ref, q_ref, *refs):
    units, out_ref, acc_ref = refs[: len(names)], refs[-2], refs[-1]
    acc_ref[...] = jnp.zeros_like(acc_ref)
    me = lax.axis_index("ctx")

    @pl.when(me < PLANE)
    def _():
        ends = history_ends(hist_ref)
        owners = [unit_owner(me, *name) for name in names]
        add_units(ends, (me + PLANE) * ROWS, q_ref, list(zip(owners, units)), acc_ref)

    out_ref[...] = acc_ref[...].astype(jnp.bfloat16)


def attend_lent(hist, q, units, names):
    return pl.pallas_call(
        functools.partial(lent_kernel, names),
        out_shape=jax.ShapeDtypeStruct((ROWS, HD), jnp.bfloat16),
        in_specs=[SMEM] + [VMEM] * (1 + len(units)),
        out_specs=VMEM,
        scratch_shapes=[pltpu.VMEM((ROWS, HD), jnp.float32)],
        cost_estimate=estimate(len(units)),
        compiler_params=params(),
    )(hist, q, *units)


def last_kernel(names, hist_ref, q_ref, *refs):
    units = refs[: len(names)]
    acc_in, lent_ref, update_ref, out_ref, acc_ref = refs[len(names) :]
    me = lax.axis_index("ctx")
    acc_ref[...] = acc_in[...]

    @pl.when(me >= PLANE)
    def _():
        acc_ref[...] += lent_ref[...].astype(jnp.float32)

    ends = history_ends(hist_ref)
    owners = [unit_owner(me, *name) for name in names]
    add_units(ends, me * ROWS, q_ref, list(zip(owners, units)), acc_ref)
    a = acc_ref[...]
    mean = jnp.mean(a * a, axis=-1, keepdims=True)
    normed = a * lax.rsqrt(mean + 1e-6)
    out_ref[...] = (normed * update_ref[...].astype(jnp.float32)).astype(jnp.bfloat16)


def attend_last(hist, q, units, names, acc, lent, update):
    return pl.pallas_call(
        functools.partial(last_kernel, names),
        out_shape=jax.ShapeDtypeStruct((ROWS, HD), jnp.bfloat16),
        in_specs=[SMEM] + [VMEM] * (4 + len(units)),
        out_specs=VMEM,
        scratch_shapes=[pltpu.VMEM((ROWS, HD), jnp.float32)],
        cost_estimate=estimate(len(units)),
        compiler_params=params(),
    )(hist, q, *units, acc, lent, update)


def project_kernel(rows_ref, w_ref, out_ref):
    rows = jnp.concatenate([rows_ref[h] for h in range(HEADS)], axis=1)
    mixed = jnp.dot(rows, w_ref[...], preferred_element_type=jnp.float32).astype(jnp.bfloat16)
    for h in range(HEADS):
        out_ref[h] = mixed[:, h * HD : (h + 1) * HD]


def project(rows, w):
    return pl.pallas_call(
        project_kernel,
        out_shape=jax.ShapeDtypeStruct((HEADS, CHUNK, HD), jnp.bfloat16),
        in_specs=[VMEM, VMEM],
        out_specs=VMEM,
        compiler_params=params(),
    )(rows, w)


UP = [(i, i + 1) for i in range(CTXS - 1)]
DOWN = [(i, i // PLANE * PLANE + (i - 1) % PLANE) for i in range(CTXS)]
LEND = [(i + PLANE, i) for i in range(PLANE)]
RETURN = [(i, i + PLANE) for i in range(PLANE)]


def body(ingest, src_shard, src_slot, hist_len, w_out):
    ingested, shards, slots = ingest[0, 0], src_shard[0], src_slot[0]
    move = functools.partial(lax.ppermute, axis_name="ctx")

    def to_owners(kinds):
        blocks = pick(shards, slots, ingested, kinds)
        return lax.all_to_all(blocks, "batch", split_axis=0, concat_axis=0, tiled=True)

    whole_w = lax.all_gather(w_out, "head", axis=0, tiled=True)
    (own,) = in_order(shards, to_owners((1, 2)), False)
    q, update = in_order(shards, to_owners((0, 3)), True)
    up, down = [own], [own]
    for step in range(4):
        up.append(move(up[-1], perm=UP))
        if step < 3:
            down.append(move(down[-1], perm=DOWN))
    lent_q = move(q, perm=LEND)
    acc = attend(hist_len, q, (own, up[1], down[1]), (("up", 0), ("up", 1), ("down", 1)))
    acc = attend(hist_len, q, (up[2], down[2]), (("up", 2), ("down", 2)), acc)
    lent = attend_lent(hist_len, lent_q, tuple(down), tuple(("down", k) for k in range(4)))
    lent = move(lent, perm=RETURN)
    acc = attend(hist_len, q, (up[3], down[3]), (("up", 3), ("down", 3)), acc)
    gated = attend_last(hist_len, q, (up[4],), (("up", 4),), acc, lent, update)
    rows = lax.all_to_all(gated.reshape(HEADS, CHUNK, HD), "head", 0, 0, tiled=True)
    mixed = project(rows, whole_w)
    mixed = lax.all_to_all(mixed, "head", 0, 0, tiled=True)
    return mixed.reshape(1, ROWS, HD)


def solution(mesh):
    in_specs = (
        P("ctx", "batch", None, None, None, "head"),
        P("ctx", None, None),
        P("ctx", None, None),
        P("batch", None),
        P("head", None),
    )
    out_specs = P("batch", "ctx", "head")
    return jax.shard_map(body, mesh=mesh, in_specs=in_specs, out_specs=out_specs, check_vma=False)
```

```python
import functools
import math

import jax
import jax.numpy as jnp
from jax import lax
from jax.experimental import pallas as pl
from jax.experimental.pallas import tpu as pltpu
from jax.sharding import PartitionSpec as P

HD = 128
BLOCK = 128
PER_OWNER = 6
CAPACITY = 3
GROUPS = 4
CTXS = 16
PLANE = 8
HEADS = 8
ROWS = BLOCK * PER_OWNER
CHUNK = ROWS // HEADS
TILE = 256
HALF_SCALE = 0.5 / math.sqrt(HD)
VMEM = pl.BlockSpec(memory_space=pltpu.VMEM)
SMEM = pl.BlockSpec(memory_space=pltpu.SMEM)
ANY = pl.BlockSpec(memory_space=pl.ANY)


def params(mib=16):
    return pltpu.CompilerParams(vmem_limit_bytes=mib * 1024 * 1024)


def pick_kernel(shard_ref, slot_ref, ingest_ref, out_ref, buf, sems):
    me = lax.axis_index("batch")
    copies = []
    for g in range(GROUPS):
        seen = jnp.int32(0)
        slots = [jnp.int32(0)] * CAPACITY
        for k in range(PER_OWNER):
            hit = shard_ref[g, k] == me
            slot = slot_ref[g, k]
            for r in range(CAPACITY):
                slots[r] = jnp.where(hit & (seen == r), slot, slots[r])
            seen = seen + hit.astype(jnp.int32)
        for r in range(CAPACITY):
            at = g * CAPACITY + r
            copy = pltpu.make_async_copy(ingest_ref.at[slots[r]], buf.at[at], sems.at[at])
            copy.start()
            copies.append(copy)
    for at, copy in enumerate(copies):
        copy.wait()
        out_ref[at] = buf[at].reshape(BLOCK, 4 * HD)


def pick(shards, slots, ingested):
    count = GROUPS * CAPACITY
    return pl.pallas_call(
        pick_kernel,
        out_shape=jax.ShapeDtypeStruct((count, BLOCK, 4 * HD), jnp.bfloat16),
        in_specs=[SMEM, SMEM, ANY],
        out_specs=VMEM,
        scratch_shapes=[
            pltpu.VMEM((count, BLOCK, 4, HD), jnp.bfloat16),
            pltpu.SemaphoreType.DMA((count,)),
        ],
        compiler_params=params(56),
    )(shards, slots, ingested)


def order_kernel(shard_ref, in_ref, unit_ref, query_ref, update_ref):
    me = lax.axis_index("batch")
    shards = [shard_ref[me, k] for k in range(PER_OWNER)]
    for k in range(PER_OWNER):
        rank = jnp.int32(0)
        for earlier in range(k):
            rank = rank + (shards[earlier] == shards[k]).astype(jnp.int32)
        at = shards[k] * CAPACITY + rank
        rows = slice(k * BLOCK, (k + 1) * BLOCK)
        query_ref[rows, :] = in_ref[at, :, :HD]
        unit_ref[rows, :] = in_ref[at, :, HD : 3 * HD]
        update_ref[rows, :] = in_ref[at, :, 3 * HD :]


def in_order(shards, blocks):
    shape = jax.ShapeDtypeStruct((ROWS, HD), jnp.bfloat16)
    return pl.pallas_call(
        order_kernel,
        out_shape=[jax.ShapeDtypeStruct((ROWS, 2 * HD), jnp.bfloat16), shape, shape],
        in_specs=[SMEM, VMEM],
        out_specs=[VMEM] * 3,
        compiler_params=params(),
    )(shards, blocks)


def unit_owner(me, kind, step):
    if kind == "up":
        return me - step
    plane, row = me // PLANE, me % PLANE
    return plane * PLANE + (row + step) % PLANE


def history_ends(hist_ref):
    ends, total = [], jnp.int32(0)
    for u in range(4):
        total = total + hist_ref[0, u]
        ends.append(total)
    return ends


def start_of(ends, pos):
    start = jnp.zeros_like(pos)
    for e in ends:
        start = jnp.where(pos >= e, jnp.maximum(start, e), start)
    return start


def silu_of_dot(q, k):
    s = lax.dot_general(q, k, (((1,), (1,)), ((), ())), preferred_element_type=jnp.float32)
    h = s * HALF_SCALE
    return h + h * jnp.tanh(h)


def add_units(ends, q_base, q_ref, units, acc_ref):
    def row_tile(t, _):
        rows = pl.ds(pl.multiple_of(t * TILE, TILE), TILE)
        first = q_base + t * TILE
        last = first + TILE - 1
        low, high = start_of(ends, first), start_of(ends, last)
        for owner, unit in units:
            base = owner * ROWS
            some = (base <= last) & (base + ROWS - 1 >= low)
            whole = (base + ROWS - 1 <= first) & (base >= high)

            @pl.when(whole)
            def _():
                w = silu_of_dot(q_ref[rows, :], unit[:, :HD]).astype(jnp.bfloat16)
                acc_ref[rows, :] += jnp.dot(w, unit[:, HD:], preferred_element_type=jnp.float32)

            @pl.when(some & jnp.logical_not(whole))
            def _():
                for part in range(ROWS // TILE):
                    k_first = base + part * TILE
                    keys = slice(part * TILE, (part + 1) * TILE)

                    @pl.when((k_first <= last) & (k_first + TILE - 1 >= low))
                    def _():
                        pos = first + lax.broadcasted_iota(jnp.int32, (TILE, TILE), 0)
                        key = k_first + lax.broadcasted_iota(jnp.int32, (TILE, TILE), 1)
                        seen = (key <= pos) & (key >= start_of(ends, pos))
                        w = silu_of_dot(q_ref[rows, :], unit[keys, :HD])
                        w = jnp.where(seen, w, 0.0).astype(jnp.bfloat16)
                        acc_ref[rows, :] += jnp.dot(
                            w, unit[keys, HD:], preferred_element_type=jnp.float32
                        )

        return 0

    lax.fori_loop(0, ROWS // TILE, row_tile, 0)


def attend_kernel(names, first, hist_ref, q_ref, *refs):
    units, refs = refs[: len(names)], refs[len(names) :]
    acc_ref = refs[-1]
    if first:
        acc_ref[...] = jnp.zeros_like(acc_ref)
    else:
        acc_ref[...] = refs[0][...]
    me = lax.axis_index("ctx")
    ends = history_ends(hist_ref)
    owners = [unit_owner(me, *name) for name in names]
    add_units(ends, me * ROWS, q_ref, list(zip(owners, units)), acc_ref)


def estimate(units):
    return pl.CostEstimate(
        flops=4 * ROWS * ROWS * HD * units, bytes_accessed=1 << 20, transcendentals=ROWS * ROWS * units
    )


def attend(hist, q, units, names, acc=None):
    first = acc is None
    return pl.pallas_call(
        functools.partial(attend_kernel, names, first),
        out_shape=jax.ShapeDtypeStruct((ROWS, HD), jnp.float32),
        in_specs=[SMEM] + [VMEM] * (1 + len(units) + (0 if first else 1)),
        out_specs=VMEM,
        cost_estimate=estimate(len(units)),
        compiler_params=params(),
    )(hist, q, *units, *(() if first else (acc,)))


def lent_kernel(names, first, final, hist_ref, q_ref, *refs):
    units, refs = refs[: len(names)], refs[len(names) :]
    acc_ref = refs[-1]
    if first:
        acc_ref[...] = jnp.zeros_like(acc_ref)
    else:
        acc_ref[...] = refs[0][...]
    me = lax.axis_index("ctx")

    @pl.when(me < PLANE)
    def _():
        ends = history_ends(hist_ref)
        owners = [unit_owner(me, *name) for name in names]
        add_units(ends, (me + PLANE) * ROWS, q_ref, list(zip(owners, units)), acc_ref)

    if final:
        refs[-2][...] = acc_ref[...].astype(jnp.bfloat16)


def attend_lent(hist, q, units, names, acc=None, final=False):
    first = acc is None
    return pl.pallas_call(
        functools.partial(lent_kernel, names, first, final),
        out_shape=jax.ShapeDtypeStruct((ROWS, HD), jnp.bfloat16 if final else jnp.float32),
        in_specs=[SMEM] + [VMEM] * (1 + len(units) + (0 if first else 1)),
        out_specs=VMEM,
        scratch_shapes=[pltpu.VMEM((ROWS, HD), jnp.float32)] if final else [],
        cost_estimate=estimate(len(units)),
        compiler_params=params(),
    )(hist, q, *units, *(() if first else (acc,)))


def last_kernel(names, hist_ref, q_ref, *refs):
    units = refs[: len(names)]
    acc_in, lent_ref, update_ref, out_ref, acc_ref = refs[len(names) :]
    me = lax.axis_index("ctx")
    acc_ref[...] = acc_in[...]

    @pl.when(me >= PLANE)
    def _():
        acc_ref[...] += lent_ref[...].astype(jnp.float32)

    ends = history_ends(hist_ref)
    owners = [unit_owner(me, *name) for name in names]
    add_units(ends, me * ROWS, q_ref, list(zip(owners, units)), acc_ref)
    a = acc_ref[...]
    mean = jnp.mean(a * a, axis=-1, keepdims=True)
    normed = a * lax.rsqrt(mean + 1e-6)
    out_ref[...] = (normed * update_ref[...].astype(jnp.float32)).astype(jnp.bfloat16)


def attend_last(hist, q, units, names, acc, lent, update):
    return pl.pallas_call(
        functools.partial(last_kernel, names),
        out_shape=jax.ShapeDtypeStruct((ROWS, HD), jnp.bfloat16),
        in_specs=[SMEM] + [VMEM] * (4 + len(units)),
        out_specs=VMEM,
        scratch_shapes=[pltpu.VMEM((ROWS, HD), jnp.float32)],
        cost_estimate=estimate(len(units)),
        compiler_params=params(),
    )(hist, q, *units, acc, lent, update)


def project_kernel(rows_ref, same_ref, other_ref, out_ref):
    me = lax.axis_index("head")
    total = 0.0
    for first, w_ref in ((me, same_ref), (me + 1 - 2 * (me % 2), other_ref)):
        heads = [rows_ref[(first + ahead) % HEADS] for ahead in (0, HEADS - 2, 2, 4)]
        rows = jnp.concatenate(heads, axis=1)
        total = total + jnp.dot(rows, w_ref[...], preferred_element_type=jnp.float32)
    mixed = total.astype(jnp.bfloat16)
    for h in range(HEADS):
        out_ref[h] = mixed[:, h * HD : (h + 1) * HD]


def project(rows, same, other):
    return pl.pallas_call(
        project_kernel,
        out_shape=jax.ShapeDtypeStruct((HEADS, CHUNK, HD), jnp.bfloat16),
        in_specs=[VMEM] * 3,
        out_specs=VMEM,
        compiler_params=params(),
    )(rows, same, other)


X_UP = [(h, (h + 2) % HEADS) for h in range(HEADS)]
X_DOWN = [(h, (h - 2) % HEADS) for h in range(HEADS)]
CORE = [(h, h ^ 1) for h in range(HEADS)]
UP = [(i, i + 1) for i in range(CTXS - 1)]
DOWN = [(i, i // PLANE * PLANE + (i - 1) % PLANE) for i in range(CTXS)]
LEND = [(i + PLANE, i) for i in range(PLANE)]
RETURN = [(i, i + PLANE) for i in range(PLANE)]


def body(ingest, src_shard, src_slot, hist_len, w_out):
    ingested, shards, slots = ingest[0, 0], src_shard[0], src_slot[0]
    move = functools.partial(lax.ppermute, axis_name="ctx")

    def to_all(x):
        return lax.all_to_all(x, "head", 0, 0, tiled=True)

    blocks = pick(shards, slots, ingested)
    w_late, blocks = lax.optimization_barrier((w_out, blocks))
    arrived = lax.all_to_all(blocks, "batch", split_axis=0, concat_axis=0, tiled=True)
    cross = functools.partial(lax.ppermute, axis_name="head")
    half = HD // 2
    w_up, w_down = cross(w_late, perm=X_UP), cross(w_late, perm=X_DOWN)
    w_far = [cross(w_up[:half], perm=X_UP), cross(w_down[half:], perm=X_DOWN)]
    w_same = jnp.concatenate([w_late, w_up, w_down, *w_far])
    w_other = cross(w_same, perm=CORE)
    w_same, w_other, arrived = lax.optimization_barrier((w_same, w_other, arrived))
    own, q, update = in_order(shards, arrived)
    up, down = [own], [own]
    for step in range(4):
        up.append(move(up[-1], perm=UP))
        if step < 3:
            down.append(move(down[-1], perm=DOWN))
    lent_q = move(q, perm=LEND)
    acc = attend(hist_len, q, (own,), (("up", 0),))
    acc = attend(hist_len, q, (up[1], down[1]), (("up", 1), ("down", 1)), acc)
    lent = attend_lent(hist_len, lent_q, tuple(down[:2]), (("down", 0), ("down", 1)))
    acc = attend(hist_len, q, (up[2], down[2]), (("up", 2), ("down", 2)), acc)
    lent = attend_lent(
        hist_len, lent_q, tuple(down[2:]), (("down", 2), ("down", 3)), lent, final=True
    )
    lent = move(lent, perm=RETURN)
    acc = attend(hist_len, q, (up[3], down[3]), (("up", 3), ("down", 3)), acc)
    gated = attend_last(hist_len, q, (up[4],), (("up", 4),), acc, lent, update)
    rows = to_all(gated.reshape(HEADS, CHUNK, HD))
    mixed = to_all(project(rows, w_same, w_other))
    return mixed.reshape(1, ROWS, HD)


def solution(mesh):
    in_specs = (
        P("ctx", "batch", None, None, None, "head"),
        P("ctx", None, None),
        P("ctx", None, None),
        P("batch", None),
        P("head", None),
    )
    out_specs = P("batch", "ctx", "head")
    return jax.shard_map(body, mesh=mesh, in_specs=in_specs, out_specs=out_specs, check_vma=False)
```

```python
import functools
import math

import jax
import jax.numpy as jnp
from jax import lax
from jax.experimental import pallas as pl
from jax.experimental.pallas import tpu as pltpu
from jax.sharding import PartitionSpec as P

HD = 128
BLOCK = 128
PER_OWNER = 6
CAPACITY = 3
GROUPS = 4
CTXS = 16
PLANE = 8
HEADS = 8
ROWS = BLOCK * PER_OWNER
CHUNK = ROWS // HEADS
TILE = 256
HALF_SCALE = 0.5 / math.sqrt(HD)
VMEM = pl.BlockSpec(memory_space=pltpu.VMEM)
SMEM = pl.BlockSpec(memory_space=pltpu.SMEM)
ANY = pl.BlockSpec(memory_space=pl.ANY)


def params(mib=16):
    return pltpu.CompilerParams(vmem_limit_bytes=mib * 1024 * 1024)


def pick_kernel(shard_ref, slot_ref, ingest_ref, out_ref, buf, sems):
    me = lax.axis_index("batch")
    copies = []
    for g in range(GROUPS):
        seen = jnp.int32(0)
        slots = [jnp.int32(0)] * CAPACITY
        for k in range(PER_OWNER):
            hit = shard_ref[g, k] == me
            slot = slot_ref[g, k]
            for r in range(CAPACITY):
                slots[r] = jnp.where(hit & (seen == r), slot, slots[r])
            seen = seen + hit.astype(jnp.int32)
        for r in range(CAPACITY):
            at = g * CAPACITY + r
            copy = pltpu.make_async_copy(ingest_ref.at[slots[r]], buf.at[at], sems.at[at])
            copy.start()
            copies.append(copy)
    for at, copy in enumerate(copies):
        copy.wait()
        out_ref[at] = buf[at].reshape(BLOCK, 4 * HD)


def pick(shards, slots, ingested):
    count = GROUPS * CAPACITY
    return pl.pallas_call(
        pick_kernel,
        out_shape=jax.ShapeDtypeStruct((count, BLOCK, 4 * HD), jnp.bfloat16),
        in_specs=[SMEM, SMEM, ANY],
        out_specs=VMEM,
        scratch_shapes=[
            pltpu.VMEM((count, BLOCK, 4, HD), jnp.bfloat16),
            pltpu.SemaphoreType.DMA((count,)),
        ],
        compiler_params=params(56),
    )(shards, slots, ingested)


def order_kernel(shard_ref, in_ref, unit_ref, query_ref, update_ref):
    me = lax.axis_index("batch")
    shards = [shard_ref[me, k] for k in range(PER_OWNER)]
    for k in range(PER_OWNER):
        rank = jnp.int32(0)
        for earlier in range(k):
            rank = rank + (shards[earlier] == shards[k]).astype(jnp.int32)
        at = shards[k] * CAPACITY + rank
        rows = slice(k * BLOCK, (k + 1) * BLOCK)
        query_ref[rows, :] = in_ref[at, :, :HD]
        unit_ref[rows, :] = in_ref[at, :, HD : 3 * HD]
        update_ref[rows, :] = in_ref[at, :, 3 * HD :]


def in_order(shards, blocks):
    shape = jax.ShapeDtypeStruct((ROWS, HD), jnp.bfloat16)
    return pl.pallas_call(
        order_kernel,
        out_shape=[jax.ShapeDtypeStruct((ROWS, 2 * HD), jnp.bfloat16), shape, shape],
        in_specs=[SMEM, VMEM],
        out_specs=[VMEM] * 3,
        compiler_params=params(),
    )(shards, blocks)


def unit_owner(stream, step):
    me = lax.axis_index("ctx")
    plane, row = me // PLANE, me % PLANE
    wrapped = plane * PLANE + (row + step) % PLANE if step < 4 else -1
    return jnp.where(lax.axis_index("head") % 2 == stream, me - step, wrapped)


def history_ends(hist_ref):
    ends, total = [], jnp.int32(0)
    for u in range(4):
        total = total + hist_ref[0, u]
        ends.append(total)
    return ends


def start_of(ends, pos):
    start = jnp.zeros_like(pos)
    for e in ends:
        start = jnp.where(pos >= e, jnp.maximum(start, e), start)
    return start


def silu_of_dot(q, k):
    s = lax.dot_general(q, k, (((1,), (1,)), ((), ())), preferred_element_type=jnp.float32)
    h = s * HALF_SCALE
    return h + h * jnp.tanh(h)


def add_units(ends, q_base, q_ref, units, acc_ref):
    def row_tile(t, _):
        rows = pl.ds(pl.multiple_of(t * TILE, TILE), TILE)
        first = q_base + t * TILE
        last = first + TILE - 1
        low, high = start_of(ends, first), start_of(ends, last)
        for owner, unit in units:
            base = owner * ROWS
            some = (base <= last) & (base + ROWS - 1 >= low)
            whole = (base + ROWS - 1 <= first) & (base >= high)

            @pl.when(whole)
            def _():
                w = silu_of_dot(q_ref[rows, :], unit[:, :HD]).astype(jnp.bfloat16)
                acc_ref[rows, :] += jnp.dot(w, unit[:, HD:], preferred_element_type=jnp.float32)

            @pl.when(some & jnp.logical_not(whole))
            def _():
                for part in range(ROWS // TILE):
                    k_first = base + part * TILE
                    keys = slice(part * TILE, (part + 1) * TILE)

                    @pl.when((k_first <= last) & (k_first + TILE - 1 >= low))
                    def _():
                        pos = first + lax.broadcasted_iota(jnp.int32, (TILE, TILE), 0)
                        key = k_first + lax.broadcasted_iota(jnp.int32, (TILE, TILE), 1)
                        seen = (key <= pos) & (key >= start_of(ends, pos))
                        w = silu_of_dot(q_ref[rows, :], unit[keys, :HD])
                        w = jnp.where(seen, w, 0.0).astype(jnp.bfloat16)
                        acc_ref[rows, :] += jnp.dot(
                            w, unit[keys, HD:], preferred_element_type=jnp.float32
                        )

        return 0

    lax.fori_loop(0, ROWS // TILE, row_tile, 0)


def attend_kernel(names, first, hist_ref, q_ref, *refs):
    units, refs = refs[: len(names)], refs[len(names) :]
    acc_ref = refs[-1]
    if first:
        acc_ref[...] = jnp.zeros_like(acc_ref)
    else:
        acc_ref[...] = refs[0][...]
    me = lax.axis_index("ctx")
    ends = history_ends(hist_ref)
    owners = [unit_owner(*name) for name in names]
    add_units(ends, me * ROWS, q_ref, list(zip(owners, units)), acc_ref)


def estimate(units):
    return pl.CostEstimate(
        flops=4 * ROWS * ROWS * HD * units, bytes_accessed=1 << 20, transcendentals=ROWS * ROWS * units
    )


def attend(hist, q, units, names, acc=None):
    first = acc is None
    return pl.pallas_call(
        functools.partial(attend_kernel, names, first),
        out_shape=jax.ShapeDtypeStruct((ROWS, HD), jnp.float32),
        in_specs=[SMEM] + [VMEM] * (1 + len(units) + (0 if first else 1)),
        out_specs=VMEM,
        cost_estimate=estimate(len(units)),
        compiler_params=params(),
    )(hist, q, *units, *(() if first else (acc,)))


def lent_kernel(names, first, final, hist_ref, q_ref, *refs):
    units, refs = refs[: len(names)], refs[len(names) :]
    acc_ref = refs[-1]
    if first:
        acc_ref[...] = jnp.zeros_like(acc_ref)
    else:
        acc_ref[...] = refs[0][...]
    me = lax.axis_index("ctx")

    @pl.when(me < PLANE)
    def _():
        ends = history_ends(hist_ref)
        owners = [unit_owner(*name) for name in names]
        add_units(ends, (me + PLANE) * ROWS, q_ref, list(zip(owners, units)), acc_ref)

    if final:
        refs[-2][...] = acc_ref[...].astype(jnp.bfloat16)


def attend_lent(hist, q, units, names, acc=None, final=False):
    first = acc is None
    return pl.pallas_call(
        functools.partial(lent_kernel, names, first, final),
        out_shape=jax.ShapeDtypeStruct((ROWS, HD), jnp.bfloat16 if final else jnp.float32),
        in_specs=[SMEM] + [VMEM] * (1 + len(units) + (0 if first else 1)),
        out_specs=VMEM,
        scratch_shapes=[pltpu.VMEM((ROWS, HD), jnp.float32)] if final else [],
        cost_estimate=estimate(len(units)),
        compiler_params=params(),
    )(hist, q, *units, *(() if first else (acc,)))


def last_kernel(names, hist_ref, q_ref, *refs):
    units = refs[: len(names)]
    acc_in, lent_ref, update_ref, out_ref, acc_ref = refs[len(names) :]
    me = lax.axis_index("ctx")
    acc_ref[...] = acc_in[...]

    @pl.when(me >= PLANE)
    def _():
        acc_ref[...] += lent_ref[...].astype(jnp.float32)

    ends = history_ends(hist_ref)
    owners = [unit_owner(*name) for name in names]
    add_units(ends, me * ROWS, q_ref, list(zip(owners, units)), acc_ref)
    a = acc_ref[...]
    mean = jnp.mean(a * a, axis=-1, keepdims=True)
    normed = a * lax.rsqrt(mean + 1e-6)
    out_ref[...] = (normed * update_ref[...].astype(jnp.float32)).astype(jnp.bfloat16)


def attend_last(hist, q, units, names, acc, lent, update):
    return pl.pallas_call(
        functools.partial(last_kernel, names),
        out_shape=jax.ShapeDtypeStruct((ROWS, HD), jnp.bfloat16),
        in_specs=[SMEM] + [VMEM] * (4 + len(units)),
        out_specs=VMEM,
        scratch_shapes=[pltpu.VMEM((ROWS, HD), jnp.float32)],
        cost_estimate=estimate(len(units)),
        compiler_params=params(),
    )(hist, q, *units, acc, lent, update)


def project_kernel(rows_ref, own_ref, partner_ref, mine_ref, theirs_ref, out_ref):
    me = lax.axis_index("head")
    partner = me + 1 - 2 * (me % 2)
    total = jnp.dot(rows_ref[me], own_ref[...], preferred_element_type=jnp.float32)
    total += jnp.dot(rows_ref[partner], partner_ref[...], preferred_element_type=jnp.float32)
    for first, other, w_ref in ((me, partner, mine_ref), (partner, me, theirs_ref)):
        ahead = HEADS - 2 + 4 * (first % 2)
        heads = ((first + ahead) % HEADS, (other + ahead) % HEADS, (first + 4) % HEADS)
        rows = jnp.concatenate([rows_ref[h] for h in heads], axis=1)
        total += jnp.dot(rows, w_ref[...], preferred_element_type=jnp.float32)
    mixed = total.astype(jnp.bfloat16)
    for h in range(HEADS):
        out_ref[h] = mixed[:, h * HD : (h + 1) * HD]


def project(rows, *w):
    return pl.pallas_call(
        project_kernel,
        out_shape=jax.ShapeDtypeStruct((HEADS, CHUNK, HD), jnp.bfloat16),
        in_specs=[VMEM] * (1 + len(w)),
        out_specs=VMEM,
        compiler_params=params(),
    )(rows, *w)


CORE = [(h, h ^ 1) for h in range(HEADS)]
X_TURN = [(h, (h + 2 - 4 * (h % 2)) % HEADS) for h in range(HEADS)]
UP = [(i, i + 1) for i in range(CTXS - 1)]
DOWN = [(i, i // PLANE * PLANE + (i - 1) % PLANE) for i in range(CTXS)]
LEND = [(i + PLANE, i) for i in range(PLANE)]
RETURN = [(i, i + PLANE) for i in range(PLANE)]


def stream_pairs(stream, step):
    pairs = []
    for h in range(HEADS):
        moves = UP if h % 2 == stream else DOWN if step < 4 else []
        pairs += [(i * HEADS + h, j * HEADS + h) for i, j in moves]
    return pairs


def gather_w(w):
    cross = functools.partial(lax.ppermute, axis_name="head")
    partner = cross(w, perm=CORE)
    near = cross(jnp.concatenate([w, partner]), perm=X_TURN)
    mine = jnp.concatenate([near, cross(near[:HD], perm=X_TURN)])
    return w, partner, mine, cross(mine, perm=CORE)


def body(ingest, src_shard, src_slot, hist_len, w_out):
    ingested, shards, slots = ingest[0, 0], src_shard[0], src_slot[0]
    move = functools.partial(lax.ppermute, axis_name="ctx")

    def to_all(x):
        return lax.all_to_all(x, "head", 0, 0, tiled=True)

    blocks = pick(shards, slots, ingested)
    w_late, blocks = lax.optimization_barrier((w_out, blocks))
    arrived = lax.all_to_all(blocks, "batch", split_axis=0, concat_axis=0, tiled=True)
    whole_w, arrived = lax.optimization_barrier((gather_w(w_late), arrived))
    own, q, update = in_order(shards, arrived)
    units = [(own,)]
    last = [own, own]
    for step in range(1, 5):
        last = [
            lax.ppermute(last[stream], ("ctx", "head"), stream_pairs(stream, step))
            for stream in range(2)
        ]
        units.append(tuple(last))
    names = [((0, 0),)] + [((0, step), (1, step)) for step in range(1, 5)]
    lent_q = move(q, perm=LEND)
    acc = attend(hist_len, q, units[0], names[0])
    acc = attend(hist_len, q, units[1], names[1], acc)
    lent = attend_lent(hist_len, lent_q, units[0] + units[1], names[0] + names[1])
    acc = attend(hist_len, q, units[2], names[2], acc)
    lent = attend_lent(
        hist_len, lent_q, units[2] + units[3], names[2] + names[3], lent, final=True
    )
    lent = move(lent, perm=RETURN)
    acc = attend(hist_len, q, units[3], names[3], acc)
    gated = attend_last(hist_len, q, units[4], names[4], acc, lent, update)
    rows = to_all(gated.reshape(HEADS, CHUNK, HD))
    mixed = to_all(project(rows, *whole_w))
    return mixed.reshape(1, ROWS, HD)


def solution(mesh):
    in_specs = (
        P("ctx", "batch", None, None, None, "head"),
        P("ctx", None, None),
        P("ctx", None, None),
        P("batch", None),
        P("head", None),
    )
    out_specs = P("batch", "ctx", "head")
    return jax.shard_map(body, mesh=mesh, in_specs=in_specs, out_specs=out_specs, check_vma=False)
```

```python
import functools
import math

import jax
import jax.numpy as jnp
from jax import lax
from jax.experimental import pallas as pl
from jax.experimental.pallas import tpu as pltpu
from jax.sharding import PartitionSpec as P

HD = 128
BLOCK = 128
PER_OWNER = 6
CAPACITY = 3
GROUPS = 4
CTXS = 16
PLANE = 8
HEADS = 8
ROWS = BLOCK * PER_OWNER
CHUNK = ROWS // HEADS
TILE = 256
HALF_SCALE = 0.5 / math.sqrt(HD)
VMEM = pl.BlockSpec(memory_space=pltpu.VMEM)
SMEM = pl.BlockSpec(memory_space=pltpu.SMEM)
ANY = pl.BlockSpec(memory_space=pl.ANY)


def params(mib=16):
    return pltpu.CompilerParams(vmem_limit_bytes=mib * 1024 * 1024)


def pick_kernel(shard_ref, slot_ref, ingest_ref, out_ref, buf, sems):
    me = lax.axis_index("batch")
    copies = []
    for g in range(GROUPS):
        seen = jnp.int32(0)
        slots = [jnp.int32(0)] * CAPACITY
        for k in range(PER_OWNER):
            hit = shard_ref[g, k] == me
            slot = slot_ref[g, k]
            for r in range(CAPACITY):
                slots[r] = jnp.where(hit & (seen == r), slot, slots[r])
            seen = seen + hit.astype(jnp.int32)
        for r in range(CAPACITY):
            at = g * CAPACITY + r
            copy = pltpu.make_async_copy(ingest_ref.at[slots[r]], buf.at[at], sems.at[at])
            copy.start()
            copies.append(copy)
    for at, copy in enumerate(copies):
        copy.wait()
        out_ref[at] = buf[at].reshape(BLOCK, 4 * HD)


def pick(shards, slots, ingested):
    count = GROUPS * CAPACITY
    return pl.pallas_call(
        pick_kernel,
        out_shape=jax.ShapeDtypeStruct((count, BLOCK, 4 * HD), jnp.bfloat16),
        in_specs=[SMEM, SMEM, ANY],
        out_specs=VMEM,
        scratch_shapes=[
            pltpu.VMEM((count, BLOCK, 4, HD), jnp.bfloat16),
            pltpu.SemaphoreType.DMA((count,)),
        ],
        compiler_params=params(56),
    )(shards, slots, ingested)


def order_kernel(shard_ref, in_ref, unit_ref, query_ref, update_ref):
    me = lax.axis_index("batch")
    shards = [shard_ref[me, k] for k in range(PER_OWNER)]
    for k in range(PER_OWNER):
        rank = jnp.int32(0)
        for earlier in range(k):
            rank = rank + (shards[earlier] == shards[k]).astype(jnp.int32)
        at = shards[k] * CAPACITY + rank
        rows = slice(k * BLOCK, (k + 1) * BLOCK)
        query_ref[rows, :] = in_ref[at, :, :HD]
        unit_ref[rows, :] = in_ref[at, :, HD : 3 * HD]
        update_ref[rows, :] = in_ref[at, :, 3 * HD :]


def in_order(shards, blocks):
    shape = jax.ShapeDtypeStruct((ROWS, HD), jnp.bfloat16)
    return pl.pallas_call(
        order_kernel,
        out_shape=[jax.ShapeDtypeStruct((ROWS, 2 * HD), jnp.bfloat16), shape, shape],
        in_specs=[SMEM, VMEM],
        out_specs=[VMEM] * 3,
        compiler_params=params(),
    )(shards, blocks)


def unit_owner(stream, step):
    me = lax.axis_index("ctx")
    plane, row = me // PLANE, me % PLANE
    wrapped = plane * PLANE + (row + step) % PLANE if step < 4 else -1
    return jnp.where((row + stream) % 2 == 1, me - step, wrapped)


def history_ends(hist_ref):
    ends, total = [], jnp.int32(0)
    for u in range(4):
        total = total + hist_ref[0, u]
        ends.append(total)
    return ends


def start_of(ends, pos):
    start = jnp.zeros_like(pos)
    for e in ends:
        start = jnp.where(pos >= e, jnp.maximum(start, e), start)
    return start


def silu_of_dot(q, k):
    s = lax.dot_general(q, k, (((1,), (1,)), ((), ())), preferred_element_type=jnp.float32)
    h = s * HALF_SCALE
    return h + h * jnp.tanh(h)


def add_units(ends, q_base, q_ref, units, acc_ref):
    def row_tile(t, _):
        rows = pl.ds(pl.multiple_of(t * TILE, TILE), TILE)
        first = q_base + t * TILE
        last = first + TILE - 1
        low, high = start_of(ends, first), start_of(ends, last)
        for owner, unit in units:
            base = owner * ROWS
            some = (base <= last) & (base + ROWS - 1 >= low)
            whole = (base + ROWS - 1 <= first) & (base >= high)

            @pl.when(whole)
            def _():
                w = silu_of_dot(q_ref[rows, :], unit[:, :HD]).astype(jnp.bfloat16)
                acc_ref[rows, :] += jnp.dot(w, unit[:, HD:], preferred_element_type=jnp.float32)

            @pl.when(some & jnp.logical_not(whole))
            def _():
                for part in range(ROWS // TILE):
                    k_first = base + part * TILE
                    keys = slice(part * TILE, (part + 1) * TILE)

                    @pl.when((k_first <= last) & (k_first + TILE - 1 >= low))
                    def _():
                        pos = first + lax.broadcasted_iota(jnp.int32, (TILE, TILE), 0)
                        key = k_first + lax.broadcasted_iota(jnp.int32, (TILE, TILE), 1)
                        seen = (key <= pos) & (key >= start_of(ends, pos))
                        w = silu_of_dot(q_ref[rows, :], unit[keys, :HD])
                        w = jnp.where(seen, w, 0.0).astype(jnp.bfloat16)
                        acc_ref[rows, :] += jnp.dot(
                            w, unit[keys, HD:], preferred_element_type=jnp.float32
                        )

        return 0

    lax.fori_loop(0, ROWS // TILE, row_tile, 0)


def attend_kernel(names, first, hist_ref, q_ref, *refs):
    units, refs = refs[: len(names)], refs[len(names) :]
    acc_ref = refs[-1]
    if first:
        acc_ref[...] = jnp.zeros_like(acc_ref)
    else:
        acc_ref[...] = refs[0][...]
    me = lax.axis_index("ctx")
    ends = history_ends(hist_ref)
    owners = [unit_owner(*name) for name in names]
    add_units(ends, me * ROWS, q_ref, list(zip(owners, units)), acc_ref)


def estimate(units):
    return pl.CostEstimate(
        flops=4 * ROWS * ROWS * HD * units, bytes_accessed=1 << 20, transcendentals=ROWS * ROWS * units
    )


def attend(hist, q, units, names, acc=None):
    first = acc is None
    return pl.pallas_call(
        functools.partial(attend_kernel, names, first),
        out_shape=jax.ShapeDtypeStruct((ROWS, HD), jnp.float32),
        in_specs=[SMEM] + [VMEM] * (1 + len(units) + (0 if first else 1)),
        out_specs=VMEM,
        cost_estimate=estimate(len(units)),
        compiler_params=params(),
    )(hist, q, *units, *(() if first else (acc,)))


def lent_kernel(names, first, final, hist_ref, q_ref, *refs):
    units, refs = refs[: len(names)], refs[len(names) :]
    acc_ref = refs[-1]
    if first:
        acc_ref[...] = jnp.zeros_like(acc_ref)
    else:
        acc_ref[...] = refs[0][...]
    me = lax.axis_index("ctx")

    @pl.when(me < PLANE)
    def _():
        ends = history_ends(hist_ref)
        owners = [unit_owner(*name) for name in names]
        add_units(ends, (me + PLANE) * ROWS, q_ref, list(zip(owners, units)), acc_ref)

    if final:
        refs[-2][...] = acc_ref[...].astype(jnp.bfloat16)


def attend_lent(hist, q, units, names, acc=None, final=False):
    first = acc is None
    return pl.pallas_call(
        functools.partial(lent_kernel, names, first, final),
        out_shape=jax.ShapeDtypeStruct((ROWS, HD), jnp.bfloat16 if final else jnp.float32),
        in_specs=[SMEM] + [VMEM] * (1 + len(units) + (0 if first else 1)),
        out_specs=VMEM,
        scratch_shapes=[pltpu.VMEM((ROWS, HD), jnp.float32)] if final else [],
        cost_estimate=estimate(len(units)),
        compiler_params=params(),
    )(hist, q, *units, *(() if first else (acc,)))


def last_kernel(names, hist_ref, q_ref, *refs):
    units = refs[: len(names)]
    acc_in, lent_ref, update_ref, out_ref, acc_ref = refs[len(names) :]
    me = lax.axis_index("ctx")
    acc_ref[...] = acc_in[...]

    @pl.when(me >= PLANE)
    def _():
        acc_ref[...] += lent_ref[...].astype(jnp.float32)

    ends = history_ends(hist_ref)
    owners = [unit_owner(*name) for name in names]
    add_units(ends, me * ROWS, q_ref, list(zip(owners, units)), acc_ref)
    a = acc_ref[...]
    mean = jnp.mean(a * a, axis=-1, keepdims=True)
    normed = a * lax.rsqrt(mean + 1e-6)
    out_ref[...] = (normed * update_ref[...].astype(jnp.float32)).astype(jnp.bfloat16)


def attend_last(hist, q, units, names, acc, lent, update):
    return pl.pallas_call(
        functools.partial(last_kernel, names),
        out_shape=jax.ShapeDtypeStruct((ROWS, HD), jnp.bfloat16),
        in_specs=[SMEM] + [VMEM] * (4 + len(units)),
        out_specs=VMEM,
        scratch_shapes=[pltpu.VMEM((ROWS, HD), jnp.float32)],
        cost_estimate=estimate(len(units)),
        compiler_params=params(),
    )(hist, q, *units, acc, lent, update)


def near_heads(head):
    chip, core = head // 2, head % 2
    even = chip + 1 - 2 * (chip % 2)
    odd = (chip + 3 + 2 * (chip % 2)) % 4
    return head, even * 2 + core, odd * 2 + core, (head + 4) % HEADS


def project_kernel(rows_ref, mine_ref, theirs_ref, out_ref):
    me = lax.axis_index("head")
    total = 0.0
    for head, w_ref in ((me, mine_ref), (me + 1 - 2 * (me % 2), theirs_ref)):
        rows = jnp.concatenate([rows_ref[h] for h in near_heads(head)], axis=1)
        total = total + jnp.dot(rows, w_ref[...], preferred_element_type=jnp.float32)
    mixed = total.astype(jnp.bfloat16)
    for h in range(HEADS):
        out_ref[h] = mixed[:, h * HD : (h + 1) * HD]


def project(rows, mine, theirs):
    return pl.pallas_call(
        project_kernel,
        out_shape=jax.ShapeDtypeStruct((HEADS, CHUNK, HD), jnp.bfloat16),
        in_specs=[VMEM] * 3,
        out_specs=VMEM,
        compiler_params=params(),
    )(rows, mine, theirs)


CORE = [(h, h ^ 1) for h in range(HEADS)]
X_EVEN = [(h, near_heads(h)[1]) for h in range(HEADS)]
X_ODD = [(h, near_heads(h)[2]) for h in range(HEADS)]
UP = [(i, i + 1) for i in range(CTXS - 1)]
DOWN = [(i, i // PLANE * PLANE + (i - 1) % PLANE) for i in range(CTXS)]
LEND = [(i + PLANE, i) for i in range(PLANE)]
RETURN = [(i, i + PLANE) for i in range(PLANE)]


def stream_pairs(stream, step):
    ups = [(i, j) for i, j in UP if i % 2 == stream]
    downs = [(i, j) for i, j in DOWN if i % 2 != stream]
    return ups + (downs if step < 4 else [])


def gather_w(w):
    cross = functools.partial(lax.ppermute, axis_name="head")
    half = HD // 2
    even, odd = cross(w, perm=X_EVEN), cross(w, perm=X_ODD)
    far = [cross(odd[:half], perm=X_EVEN), cross(even[half:], perm=X_ODD)]
    mine = jnp.concatenate([w, even, odd, *far])
    return mine, cross(mine, perm=CORE)


def body(ingest, src_shard, src_slot, hist_len, w_out):
    ingested, shards, slots = ingest[0, 0], src_shard[0], src_slot[0]
    move = functools.partial(lax.ppermute, axis_name="ctx")

    def to_all(x):
        return lax.all_to_all(x, "head", 0, 0, tiled=True)

    blocks = pick(shards, slots, ingested)
    w_late, blocks = lax.optimization_barrier((w_out, blocks))
    arrived = lax.all_to_all(blocks, "batch", split_axis=0, concat_axis=0, tiled=True)
    whole_w, arrived = lax.optimization_barrier((gather_w(w_late), arrived))
    own, q, update = in_order(shards, arrived)
    units = [(own,)]
    last = [own, own]
    for step in range(1, 5):
        last = [move(last[1 - stream], perm=stream_pairs(stream, step)) for stream in range(2)]
        units.append(tuple(last))
    names = [((0, 0),)] + [((0, step), (1, step)) for step in range(1, 5)]
    lent_q = move(q, perm=LEND)
    acc = attend(hist_len, q, units[0], names[0])
    acc = attend(hist_len, q, units[1], names[1], acc)
    lent = attend_lent(hist_len, lent_q, units[0] + units[1], names[0] + names[1])
    acc = attend(hist_len, q, units[2], names[2], acc)
    lent = attend_lent(
        hist_len, lent_q, units[2] + units[3], names[2] + names[3], lent, final=True
    )
    lent = move(lent, perm=RETURN)
    acc = attend(hist_len, q, units[3], names[3], acc)
    gated = attend_last(hist_len, q, units[4], names[4], acc, lent, update)
    rows = to_all(gated.reshape(HEADS, CHUNK, HD))
    mixed = to_all(project(rows, *whole_w))
    return mixed.reshape(1, ROWS, HD)


def solution(mesh):
    in_specs = (
        P("ctx", "batch", None, None, None, "head"),
        P("ctx", None, None),
        P("ctx", None, None),
        P("batch", None),
        P("head", None),
    )
    out_specs = P("batch", "ctx", "head")
    return jax.shard_map(body, mesh=mesh, in_specs=in_specs, out_specs=out_specs, check_vma=False)
```

```python
import functools
import math

import jax
import jax.numpy as jnp
from jax import lax
from jax.experimental import pallas as pl
from jax.experimental.pallas import tpu as pltpu
from jax.sharding import PartitionSpec as P

HD = 128
BLOCK = 128
PER_OWNER = 6
CAPACITY = 3
GROUPS = 4
CTXS = 16
PLANE = 8
HEADS = 8
ROWS = BLOCK * PER_OWNER
CHUNK = ROWS // HEADS
TILE = 256
WEIGHT = 8
HALF_SCALE = 0.5 / math.sqrt(HD)
VMEM = pl.BlockSpec(memory_space=pltpu.VMEM)
SMEM = pl.BlockSpec(memory_space=pltpu.SMEM)
ANY = pl.BlockSpec(memory_space=pl.ANY)


def params(mib=16):
    return pltpu.CompilerParams(vmem_limit_bytes=mib * 1024 * 1024)


def pick_kernel(shard_ref, slot_ref, ingest_ref, first_ref, update_ref, buf, sems):
    me = lax.axis_index("batch")
    copies = []
    for g in range(GROUPS):
        seen = jnp.int32(0)
        slots = [jnp.int32(0)] * CAPACITY
        for k in range(PER_OWNER):
            hit = shard_ref[g, k] == me
            slot = slot_ref[g, k]
            for r in range(CAPACITY):
                slots[r] = jnp.where(hit & (seen == r), slot, slots[r])
            seen = seen + hit.astype(jnp.int32)
        for r in range(CAPACITY):
            at = g * CAPACITY + r
            copy = pltpu.make_async_copy(ingest_ref.at[slots[r]], buf.at[at], sems.at[at])
            copy.start()
            copies.append(copy)
    for at, copy in enumerate(copies):
        copy.wait()
        flat = buf[at].reshape(BLOCK, 4 * HD)
        first_ref[at] = flat[:, : 3 * HD]
        update_ref[at] = flat[:, 3 * HD :]


def pick(shards, slots, ingested):
    count = GROUPS * CAPACITY
    return pl.pallas_call(
        pick_kernel,
        out_shape=[
            jax.ShapeDtypeStruct((count, BLOCK, 3 * HD), jnp.bfloat16),
            jax.ShapeDtypeStruct((count, BLOCK, HD), jnp.bfloat16),
        ],
        in_specs=[SMEM, SMEM, ANY],
        out_specs=[VMEM] * 2,
        scratch_shapes=[
            pltpu.VMEM((count, BLOCK, 4, HD), jnp.bfloat16),
            pltpu.SemaphoreType.DMA((count,)),
        ],
        compiler_params=params(56),
    )(shards, slots, ingested)


def block_places(shard_ref):
    me = lax.axis_index("batch")
    shards = [shard_ref[me, k] for k in range(PER_OWNER)]
    for k in range(PER_OWNER):
        rank = jnp.int32(0)
        for earlier in range(k):
            rank = rank + (shards[earlier] == shards[k]).astype(jnp.int32)
        yield slice(k * BLOCK, (k + 1) * BLOCK), shards[k] * CAPACITY + rank


def order_kernel(shard_ref, in_ref, unit_ref, query_ref):
    for rows, at in block_places(shard_ref):
        query_ref[rows, :] = in_ref[at, :, :HD]
        unit_ref[rows, :] = in_ref[at, :, HD:]


def in_order(shards, blocks):
    return pl.pallas_call(
        order_kernel,
        out_shape=[
            jax.ShapeDtypeStruct((ROWS, 2 * HD), jnp.bfloat16),
            jax.ShapeDtypeStruct((ROWS, HD), jnp.bfloat16),
        ],
        in_specs=[SMEM, VMEM],
        out_specs=[VMEM] * 2,
        compiler_params=params(),
    )(shards, blocks)


def unit_owner(stream, step):
    me = lax.axis_index("ctx")
    plane, row = me // PLANE, me % PLANE
    wrapped = plane * PLANE + (row + step) % PLANE if step < 4 else -1
    return jnp.where((row + stream) % 2 == 1, me - step, wrapped)


def history_ends(hist_ref):
    ends, total = [], jnp.int32(0)
    for u in range(4):
        total = total + hist_ref[0, u]
        ends.append(total)
    return ends


def start_of(ends, pos):
    start = jnp.zeros_like(pos)
    for e in ends:
        start = jnp.where(pos >= e, jnp.maximum(start, e), start)
    return start


def silu_of_dot(q, k):
    s = lax.dot_general(q, k, (((1,), (1,)), ((), ())), preferred_element_type=jnp.float32)
    h = s * HALF_SCALE
    return h + h * jnp.tanh(h)


def add_units(ends, q_base, q_ref, units, acc_ref):
    def row_tile(t, _):
        rows = pl.ds(pl.multiple_of(t * TILE, TILE), TILE)
        first = q_base + t * TILE
        last = first + TILE - 1
        low, high = start_of(ends, first), start_of(ends, last)
        for owner, unit in units:
            base = owner * ROWS
            some = (base <= last) & (base + ROWS - 1 >= low)
            whole = (base + ROWS - 1 <= first) & (base >= high)

            @pl.when(whole)
            def _():
                w = silu_of_dot(q_ref[rows, :], unit[:, :HD]).astype(jnp.bfloat16)
                acc_ref[rows, :] += jnp.dot(w, unit[:, HD:], preferred_element_type=jnp.float32)

            @pl.when(some & jnp.logical_not(whole))
            def _():
                for part in range(ROWS // TILE):
                    k_first = base + part * TILE
                    keys = slice(part * TILE, (part + 1) * TILE)

                    @pl.when((k_first <= last) & (k_first + TILE - 1 >= low))
                    def _():
                        pos = first + lax.broadcasted_iota(jnp.int32, (TILE, TILE), 0)
                        key = k_first + lax.broadcasted_iota(jnp.int32, (TILE, TILE), 1)
                        seen = (key <= pos) & (key >= start_of(ends, pos))
                        w = silu_of_dot(q_ref[rows, :], unit[keys, :HD])
                        w = jnp.where(seen, w, 0.0).astype(jnp.bfloat16)
                        acc_ref[rows, :] += jnp.dot(
                            w, unit[keys, HD:], preferred_element_type=jnp.float32
                        )

        return 0

    lax.fori_loop(0, ROWS // TILE, row_tile, 0)


def attend_kernel(names, first, hand_on, hist_ref, q_ref, *refs):
    units, refs = refs[: len(names)], refs[len(names) :]
    acc_ref = refs[-2] if hand_on else refs[-1]
    if first:
        acc_ref[...] = jnp.zeros_like(acc_ref)
    else:
        acc_ref[...] = refs[0][...]
    ends = history_ends(hist_ref)
    owners = [unit_owner(*name) for name in names]
    add_units(ends, lax.axis_index("ctx") * ROWS, q_ref, list(zip(owners, units)), acc_ref)


def estimate(units):
    return pl.CostEstimate(
        flops=WEIGHT * 4 * ROWS * ROWS * HD * units,
        bytes_accessed=1 << 20,
        transcendentals=ROWS * ROWS * units,
    )


def attend(hist, q, units, names, acc=None, later=None):
    first, hand_on = acc is None, later is not None
    args = [hist, q, *units] + ([] if first else [acc])
    own = jax.ShapeDtypeStruct((ROWS, HD), jnp.float32)
    passed = [jax.ShapeDtypeStruct(later.shape, later.dtype)] if hand_on else []
    out = pl.pallas_call(
        functools.partial(attend_kernel, names, first, hand_on),
        out_shape=[own, *passed],
        in_specs=[SMEM] + [VMEM] * (len(args) - 1) + [ANY] * hand_on,
        out_specs=[VMEM] + [ANY] * hand_on,
        input_output_aliases={len(args): 1} if hand_on else {},
        cost_estimate=estimate(len(units)),
        compiler_params=params(),
    )(*args, *([later] if hand_on else []))
    return out if hand_on else out[0]


def lent_kernel(names, first, final, hist_ref, q_ref, *refs):
    units, refs = refs[: len(names)], refs[len(names) :]
    acc_ref = refs[-1]
    if first:
        acc_ref[...] = jnp.zeros_like(acc_ref)
    else:
        acc_ref[...] = refs[0][...]
    me = lax.axis_index("ctx")

    @pl.when(me < PLANE)
    def _():
        ends = history_ends(hist_ref)
        owners = [unit_owner(*name) for name in names]
        add_units(ends, (me + PLANE) * ROWS, q_ref, list(zip(owners, units)), acc_ref)

    if final:
        refs[-2][...] = acc_ref[...].astype(jnp.bfloat16)


def attend_lent(hist, q, units, names, acc=None, final=False):
    first = acc is None
    return pl.pallas_call(
        functools.partial(lent_kernel, names, first, final),
        out_shape=jax.ShapeDtypeStruct((ROWS, HD), jnp.bfloat16 if final else jnp.float32),
        in_specs=[SMEM] + [VMEM] * (1 + len(units) + (0 if first else 1)),
        out_specs=VMEM,
        scratch_shapes=[pltpu.VMEM((ROWS, HD), jnp.float32)] if final else [],
        cost_estimate=estimate(len(units)),
        compiler_params=params(),
    )(hist, q, *units, *(() if first else (acc,)))


def last_kernel(names, hist_ref, shard_ref, q_ref, *refs):
    units = refs[: len(names)]
    acc_in, lent_ref, update_ref, out_ref, acc_ref = refs[len(names) :]
    me = lax.axis_index("ctx")
    acc_ref[...] = acc_in[...]

    @pl.when(me >= PLANE)
    def _():
        acc_ref[...] += lent_ref[...].astype(jnp.float32)

    ends = history_ends(hist_ref)
    owners = [unit_owner(*name) for name in names]
    add_units(ends, me * ROWS, q_ref, list(zip(owners, units)), acc_ref)
    for rows, at in block_places(shard_ref):
        a = acc_ref[rows, :]
        mean = jnp.mean(a * a, axis=-1, keepdims=True)
        normed = a * lax.rsqrt(mean + 1e-6)
        out_ref[rows, :] = (normed * update_ref[at].astype(jnp.float32)).astype(jnp.bfloat16)


def attend_last(hist, shards, q, units, names, acc, lent, update):
    return pl.pallas_call(
        functools.partial(last_kernel, names),
        out_shape=jax.ShapeDtypeStruct((ROWS, HD), jnp.bfloat16),
        in_specs=[SMEM, SMEM] + [VMEM] * (4 + len(units)),
        out_specs=VMEM,
        scratch_shapes=[pltpu.VMEM((ROWS, HD), jnp.float32)],
        cost_estimate=estimate(len(units)),
        compiler_params=params(),
    )(hist, shards, q, *units, acc, lent, update)


def near_heads(head):
    chip, core = head // 2, head % 2
    even = chip + 1 - 2 * (chip % 2)
    odd = (chip + 3 + 2 * (chip % 2)) % 4
    return head, even * 2 + core, odd * 2 + core, (head + 4) % HEADS


def project_kernel(rows_ref, mine_ref, theirs_ref, out_ref):
    me = lax.axis_index("head")
    total = 0.0
    for head, w_ref in ((me, mine_ref), (me + 1 - 2 * (me % 2), theirs_ref)):
        rows = jnp.concatenate([rows_ref[h] for h in near_heads(head)], axis=1)
        total = total + jnp.dot(rows, w_ref[...], preferred_element_type=jnp.float32)
    mixed = total.astype(jnp.bfloat16)
    for h in range(HEADS):
        out_ref[h] = mixed[:, h * HD : (h + 1) * HD]


def project(rows, mine, theirs):
    return pl.pallas_call(
        project_kernel,
        out_shape=jax.ShapeDtypeStruct((HEADS, CHUNK, HD), jnp.bfloat16),
        in_specs=[VMEM] * 3,
        out_specs=VMEM,
        compiler_params=params(),
    )(rows, mine, theirs)


CORE = [(h, h ^ 1) for h in range(HEADS)]
X_EVEN = [(h, near_heads(h)[1]) for h in range(HEADS)]
X_ODD = [(h, near_heads(h)[2]) for h in range(HEADS)]
UP = [(i, i + 1) for i in range(CTXS - 1)]
DOWN = [(i, i // PLANE * PLANE + (i - 1) % PLANE) for i in range(CTXS)]
LEND = [(i + PLANE, i) for i in range(PLANE)]
RETURN = [(i, i + PLANE) for i in range(PLANE)]


def stream_pairs(stream, step):
    ups = [(i, j) for i, j in UP if i % 2 == stream]
    downs = [(i, j) for i, j in DOWN if i % 2 != stream]
    return ups + (downs if step < 4 else [])


def gather_w(w):
    cross = functools.partial(lax.ppermute, axis_name="head")
    half = HD // 2
    even, odd = cross(w, perm=X_EVEN), cross(w, perm=X_ODD)
    far = [cross(odd[:half], perm=X_EVEN), cross(even[half:], perm=X_ODD)]
    mine = jnp.concatenate([w, even, odd, *far])
    return mine, cross(mine, perm=CORE)


def body(ingest, src_shard, src_slot, hist_len, w_out):
    ingested, shards, slots = ingest[0, 0], src_shard[0], src_slot[0]
    move = functools.partial(lax.ppermute, axis_name="ctx")

    def to_all(x):
        return lax.all_to_all(x, "head", 0, 0, tiled=True)

    def to_owners(x):
        return lax.all_to_all(x, "batch", split_axis=0, concat_axis=0, tiled=True)

    def step_on(last, step):
        return [move(last[1 - stream], perm=stream_pairs(stream, step)) for stream in range(2)]

    tie = lax.optimization_barrier
    names = [((0, 0),)] + [((0, step), (1, step)) for step in range(1, 5)]
    blocks, updates = pick(shards, slots, ingested)
    w_late, blocks = tie((w_out, blocks))
    arrived = to_owners(blocks)
    mine, theirs = gather_w(w_late)
    mine, arrived = tie((mine, arrived))
    own, q = in_order(shards, arrived)
    first = step_on([own, own], 1)
    second = step_on(first, 2)
    third = step_on(second, 3)
    fourth = step_on(third, 4)
    lent_q = move(q, perm=LEND)
    acc, updates = attend(hist_len, q, (own,), names[0], None, updates)
    acc, updates = attend(hist_len, q, first, names[1], acc, updates)
    update = to_owners(updates)
    lent = attend_lent(hist_len, lent_q, (own, *first), names[0] + names[1])
    acc = attend(hist_len, q, second, names[2], acc)
    lent = attend_lent(hist_len, lent_q, second, names[2], lent)
    lent = attend_lent(hist_len, lent_q, third, names[3], lent, final=True)
    lent = move(lent, perm=RETURN)
    acc = attend(hist_len, q, third, names[3], acc)
    gated = attend_last(hist_len, shards, q, fourth, names[4], acc, lent, update)
    rows = to_all(gated.reshape(HEADS, CHUNK, HD))
    mixed = to_all(project(rows, mine, theirs))
    return mixed.reshape(1, ROWS, HD)


def solution(mesh):
    in_specs = (
        P("ctx", "batch", None, None, None, "head"),
        P("ctx", None, None),
        P("ctx", None, None),
        P("batch", None),
        P("head", None),
    )
    out_specs = P("batch", "ctx", "head")
    return jax.shard_map(body, mesh=mesh, in_specs=in_specs, out_specs=out_specs, check_vma=False)
```

```python
import functools
import math

import jax
import jax.numpy as jnp
from jax import lax
from jax.experimental import pallas as pl
from jax.experimental.pallas import tpu as pltpu
from jax.sharding import PartitionSpec as P

HD = 128
BLOCK = 128
PER_OWNER = 6
CAPACITY = 3
GROUPS = 4
CTXS = 16
PLANE = 8
HEADS = 8
ROWS = BLOCK * PER_OWNER
CHUNK = ROWS // HEADS
TILE = 256
WEIGHT = 8
HALF_SCALE = 0.5 / math.sqrt(HD)
VMEM = pl.BlockSpec(memory_space=pltpu.VMEM)
SMEM = pl.BlockSpec(memory_space=pltpu.SMEM)
ANY = pl.BlockSpec(memory_space=pl.ANY)


def params(mib=16):
    return pltpu.CompilerParams(vmem_limit_bytes=mib * 1024 * 1024)


def pick_kernel(shard_ref, slot_ref, ingest_ref, out_ref, buf, sems):
    me = lax.axis_index("batch")
    copies = []
    for g in range(GROUPS):
        seen = jnp.int32(0)
        slots = [jnp.int32(0)] * CAPACITY
        for k in range(PER_OWNER):
            hit = shard_ref[g, k] == me
            slot = slot_ref[g, k]
            for r in range(CAPACITY):
                slots[r] = jnp.where(hit & (seen == r), slot, slots[r])
            seen = seen + hit.astype(jnp.int32)
        for r in range(CAPACITY):
            at = g * CAPACITY + r
            copy = pltpu.make_async_copy(ingest_ref.at[slots[r]], buf.at[at], sems.at[at])
            copy.start()
            copies.append(copy)
    for at, copy in enumerate(copies):
        copy.wait()
        out_ref[at] = buf[at].reshape(BLOCK, 4 * HD)


def pick(shards, slots, ingested):
    count = GROUPS * CAPACITY
    return pl.pallas_call(
        pick_kernel,
        out_shape=jax.ShapeDtypeStruct((count, BLOCK, 4 * HD), jnp.bfloat16),
        in_specs=[SMEM, SMEM, ANY],
        out_specs=VMEM,
        scratch_shapes=[
            pltpu.VMEM((count, BLOCK, 4, HD), jnp.bfloat16),
            pltpu.SemaphoreType.DMA((count,)),
        ],
        compiler_params=params(56),
    )(shards, slots, ingested)


def block_places(shard_ref):
    me = lax.axis_index("batch")
    shards = [shard_ref[me, k] for k in range(PER_OWNER)]
    for k in range(PER_OWNER):
        rank = jnp.int32(0)
        for earlier in range(k):
            rank = rank + (shards[earlier] == shards[k]).astype(jnp.int32)
        yield slice(k * BLOCK, (k + 1) * BLOCK), shards[k] * CAPACITY + rank


def order_kernel(shard_ref, in_ref, unit_ref, query_ref, update_ref):
    for rows, at in block_places(shard_ref):
        query_ref[rows, :] = in_ref[at, :, :HD]
        unit_ref[rows, :] = in_ref[at, :, HD : 3 * HD]
        update_ref[rows, :] = in_ref[at, :, 3 * HD :]


def in_order(shards, blocks):
    shape = jax.ShapeDtypeStruct((ROWS, HD), jnp.bfloat16)
    return pl.pallas_call(
        order_kernel,
        out_shape=[jax.ShapeDtypeStruct((ROWS, 2 * HD), jnp.bfloat16), shape, shape],
        in_specs=[SMEM, VMEM],
        out_specs=[VMEM] * 3,
        compiler_params=params(),
    )(shards, blocks)


def unit_owner(stream, step):
    me = lax.axis_index("ctx")
    plane, row = me // PLANE, me % PLANE
    wrapped = plane * PLANE + (row + step) % PLANE if step < 4 else -1
    return jnp.where((row + stream) % 2 == 1, me - step, wrapped)


def history_ends(hist_ref):
    ends, total = [], jnp.int32(0)
    for u in range(4):
        total = total + hist_ref[0, u]
        ends.append(total)
    return ends


def start_of(ends, pos):
    start = jnp.zeros_like(pos)
    for e in ends:
        start = jnp.where(pos >= e, jnp.maximum(start, e), start)
    return start


def silu_of_dot(q, k):
    s = lax.dot_general(q, k, (((1,), (1,)), ((), ())), preferred_element_type=jnp.float32)
    h = s * HALF_SCALE
    return h + h * jnp.tanh(h)


def add_units(ends, q_base, q_ref, units, acc_ref):
    def row_tile(t, _):
        rows = pl.ds(pl.multiple_of(t * TILE, TILE), TILE)
        first = q_base + t * TILE
        last = first + TILE - 1
        low, high = start_of(ends, first), start_of(ends, last)
        pos = first + lax.broadcasted_iota(jnp.int32, (TILE, 1), 0)
        start = start_of(ends, pos)
        for owner, unit in units:
            base = owner * ROWS
            some = (base <= last) & (base + ROWS - 1 >= low)
            whole = (base + ROWS - 1 <= first) & (base >= high)

            @pl.when(whole)
            def _():
                w = silu_of_dot(q_ref[rows, :], unit[:, :HD]).astype(jnp.bfloat16)
                acc_ref[rows, :] += jnp.dot(w, unit[:, HD:], preferred_element_type=jnp.float32)

            @pl.when(some & jnp.logical_not(whole))
            def _():
                for part in range(ROWS // TILE):
                    k_first = base + part * TILE
                    keys = slice(part * TILE, (part + 1) * TILE)

                    @pl.when((k_first <= last) & (k_first + TILE - 1 >= low))
                    def _():
                        key = k_first + lax.broadcasted_iota(jnp.int32, (TILE, TILE), 1)
                        seen = (key <= pos) & (key >= start)
                        w = silu_of_dot(q_ref[rows, :], unit[keys, :HD])
                        w = jnp.where(seen, w, 0.0).astype(jnp.bfloat16)
                        acc_ref[rows, :] += jnp.dot(
                            w, unit[keys, HD:], preferred_element_type=jnp.float32
                        )

        return 0

    lax.fori_loop(0, ROWS // TILE, row_tile, 0)


def attend_kernel(names, first, hist_ref, q_ref, *refs):
    units, refs = refs[: len(names)], refs[len(names) :]
    acc_ref = refs[-1]
    if first:
        acc_ref[...] = jnp.zeros_like(acc_ref)
    else:
        acc_ref[...] = refs[0][...]
    me = lax.axis_index("ctx")
    ends = history_ends(hist_ref)
    owners = [unit_owner(*name) for name in names]
    add_units(ends, me * ROWS, q_ref, list(zip(owners, units)), acc_ref)


def estimate(units):
    return pl.CostEstimate(
        flops=WEIGHT * 4 * ROWS * ROWS * HD * units,
        bytes_accessed=1 << 20,
        transcendentals=ROWS * ROWS * units,
    )


def attend(hist, q, units, names, acc=None):
    first = acc is None
    return pl.pallas_call(
        functools.partial(attend_kernel, names, first),
        out_shape=jax.ShapeDtypeStruct((ROWS, HD), jnp.float32),
        in_specs=[SMEM] + [VMEM] * (1 + len(units) + (0 if first else 1)),
        out_specs=VMEM,
        cost_estimate=estimate(len(units)),
        compiler_params=params(),
    )(hist, q, *units, *(() if first else (acc,)))


def lent_kernel(names, first, final, hist_ref, q_ref, *refs):
    units, refs = refs[: len(names)], refs[len(names) :]
    acc_ref = refs[-1]
    if first:
        acc_ref[...] = jnp.zeros_like(acc_ref)
    else:
        acc_ref[...] = refs[0][...]
    me = lax.axis_index("ctx")

    @pl.when(me < PLANE)
    def _():
        ends = history_ends(hist_ref)
        owners = [unit_owner(*name) for name in names]
        add_units(ends, (me + PLANE) * ROWS, q_ref, list(zip(owners, units)), acc_ref)

    if final:
        refs[-2][...] = acc_ref[...].astype(jnp.bfloat16)


def attend_lent(hist, q, units, names, acc=None, final=False):
    first = acc is None
    return pl.pallas_call(
        functools.partial(lent_kernel, names, first, final),
        out_shape=jax.ShapeDtypeStruct((ROWS, HD), jnp.bfloat16 if final else jnp.float32),
        in_specs=[SMEM] + [VMEM] * (1 + len(units) + (0 if first else 1)),
        out_specs=VMEM,
        scratch_shapes=[pltpu.VMEM((ROWS, HD), jnp.float32)] if final else [],
        cost_estimate=estimate(len(units)),
        compiler_params=params(),
    )(hist, q, *units, *(() if first else (acc,)))


def last_kernel(names, hist_ref, q_ref, *refs):
    units = refs[: len(names)]
    acc_in, lent_ref, update_ref, out_ref, acc_ref = refs[len(names) :]
    me = lax.axis_index("ctx")
    acc_ref[...] = acc_in[...]

    @pl.when(me >= PLANE)
    def _():
        acc_ref[...] += lent_ref[...].astype(jnp.float32)

    ends = history_ends(hist_ref)
    owners = [unit_owner(*name) for name in names]
    add_units(ends, me * ROWS, q_ref, list(zip(owners, units)), acc_ref)
    a = acc_ref[...]
    mean = jnp.mean(a * a, axis=-1, keepdims=True)
    normed = a * lax.rsqrt(mean + 1e-6)
    out_ref[...] = (normed * update_ref[...].astype(jnp.float32)).astype(jnp.bfloat16)


def attend_last(hist, q, units, names, acc, lent, update):
    return pl.pallas_call(
        functools.partial(last_kernel, names),
        out_shape=jax.ShapeDtypeStruct((ROWS, HD), jnp.bfloat16),
        in_specs=[SMEM] + [VMEM] * (4 + len(units)),
        out_specs=VMEM,
        scratch_shapes=[pltpu.VMEM((ROWS, HD), jnp.float32)],
        cost_estimate=estimate(len(units)),
        compiler_params=params(),
    )(hist, q, *units, acc, lent, update)


def near_heads(head):
    chip, core = head // 2, head % 2
    even = chip + 1 - 2 * (chip % 2)
    odd = (chip + 3 + 2 * (chip % 2)) % 4
    return head, even * 2 + core, odd * 2 + core, (head + 4) % HEADS


def project_kernel(rows_ref, mine_ref, theirs_ref, out_ref):
    me = lax.axis_index("head")
    total = 0.0
    for head, w_ref in ((me, mine_ref), (me + 1 - 2 * (me % 2), theirs_ref)):
        rows = jnp.concatenate([rows_ref[h] for h in near_heads(head)], axis=1)
        total = total + jnp.dot(rows, w_ref[...], preferred_element_type=jnp.float32)
    mixed = total.astype(jnp.bfloat16)
    for h in range(HEADS):
        out_ref[h] = mixed[:, h * HD : (h + 1) * HD]


def project(rows, mine, theirs):
    return pl.pallas_call(
        project_kernel,
        out_shape=jax.ShapeDtypeStruct((HEADS, CHUNK, HD), jnp.bfloat16),
        in_specs=[VMEM] * 3,
        out_specs=VMEM,
        compiler_params=params(),
    )(rows, mine, theirs)


CORE = [(h, h ^ 1) for h in range(HEADS)]
X_EVEN = [(h, near_heads(h)[1]) for h in range(HEADS)]
X_ODD = [(h, near_heads(h)[2]) for h in range(HEADS)]
UP = [(i, i + 1) for i in range(CTXS - 1)]
DOWN = [(i, i // PLANE * PLANE + (i - 1) % PLANE) for i in range(CTXS)]
LEND = [(i + PLANE, i) for i in range(PLANE)]
RETURN = [(i, i + PLANE) for i in range(PLANE)]


def stream_pairs(stream, step):
    ups = [(i, j) for i, j in UP if i % 2 == stream]
    downs = [(i, j) for i, j in DOWN if i % 2 != stream]
    return ups + (downs if step < 4 else [])


def gather_w(w):
    cross = functools.partial(lax.ppermute, axis_name="head")
    half = HD // 2
    even, odd = cross(w, perm=X_EVEN), cross(w, perm=X_ODD)
    far = [cross(odd[:half], perm=X_EVEN), cross(even[half:], perm=X_ODD)]
    mine = jnp.concatenate([w, even, odd, *far])
    return mine, cross(mine, perm=CORE)


def body(ingest, src_shard, src_slot, hist_len, w_out):
    ingested, shards, slots = ingest[0, 0], src_shard[0], src_slot[0]
    move = functools.partial(lax.ppermute, axis_name="ctx")

    def to_all(x):
        return lax.all_to_all(x, "head", 0, 0, tiled=True)

    def step_on(last, step):
        return [move(last[1 - stream], perm=stream_pairs(stream, step)) for stream in range(2)]

    names = [((0, 0),)] + [((0, step), (1, step)) for step in range(1, 5)]
    blocks = pick(shards, slots, ingested)
    w_late, blocks = lax.optimization_barrier((w_out, blocks))
    arrived = lax.all_to_all(blocks, "batch", split_axis=0, concat_axis=0, tiled=True)
    mine, theirs = gather_w(w_late)
    mine, theirs, arrived = lax.optimization_barrier((mine, theirs, arrived))
    own, q, update = in_order(shards, arrived)
    first = step_on([own, own], 1)
    second = step_on(first, 2)
    third = step_on(second, 3)
    fourth = step_on(third, 4)
    lent_q = move(q, perm=LEND)
    acc = attend(hist_len, q, (own,), names[0])
    acc = attend(hist_len, q, first, names[1], acc)
    lent = attend_lent(hist_len, lent_q, (own, *first), names[0] + names[1])
    acc = attend(hist_len, q, second, names[2], acc)
    lent = attend_lent(hist_len, lent_q, second, names[2], lent)
    lent = attend_lent(hist_len, lent_q, third, names[3], lent, final=True)
    lent = move(lent, perm=RETURN)
    acc = attend(hist_len, q, third, names[3], acc)
    gated = attend_last(hist_len, q, fourth, names[4], acc, lent, update)
    rows = to_all(gated.reshape(HEADS, CHUNK, HD))
    mixed = to_all(project(rows, mine, theirs))
    return mixed.reshape(1, ROWS, HD)


def solution(mesh):
    in_specs = (
        P("ctx", "batch", None, None, None, "head"),
        P("ctx", None, None),
        P("ctx", None, None),
        P("batch", None),
        P("head", None),
    )
    out_specs = P("batch", "ctx", "head")
    return jax.shard_map(body, mesh=mesh, in_specs=in_specs, out_specs=out_specs, check_vma=False)
```

```python
import functools
import math

import jax
import jax.numpy as jnp
from jax import lax
from jax.experimental import pallas as pl
from jax.experimental.pallas import tpu as pltpu
from jax.sharding import PartitionSpec as P

HD = 128
BLOCK = 128
PER_OWNER = 6
CAPACITY = 3
GROUPS = 4
CTXS = 16
PLANE = 8
HEADS = 8
ROWS = BLOCK * PER_OWNER
CHUNK = ROWS // HEADS
TILE = 256
WEIGHT = 8
HALF_SCALE = 0.5 / math.sqrt(HD)
VMEM = pl.BlockSpec(memory_space=pltpu.VMEM)
SMEM = pl.BlockSpec(memory_space=pltpu.SMEM)
ANY = pl.BlockSpec(memory_space=pl.ANY)


def params(mib=16):
    return pltpu.CompilerParams(vmem_limit_bytes=mib * 1024 * 1024)


def pick_kernel(shard_ref, slot_ref, ingest_ref, kvq_ref, *refs):
    update_refs, buf, sems = refs[:GROUPS], refs[-2], refs[-1]
    me = lax.axis_index("batch")
    copies = []
    for g in range(GROUPS):
        seen = jnp.int32(0)
        slots = [jnp.int32(0)] * CAPACITY
        for k in range(PER_OWNER):
            hit = shard_ref[g, k] == me
            slot = slot_ref[g, k]
            for r in range(CAPACITY):
                slots[r] = jnp.where(hit & (seen == r), slot, slots[r])
            seen = seen + hit.astype(jnp.int32)
        for r in range(CAPACITY):
            at = g * CAPACITY + r
            copy = pltpu.make_async_copy(ingest_ref.at[slots[r]], buf.at[at], sems.at[at])
            copy.start()
            copies.append(copy)
    for at, copy in enumerate(copies):
        copy.wait()
        kvq_ref[at] = buf[at].reshape(BLOCK, 4 * HD)[:, : 3 * HD]
    for ahead, update_ref in enumerate(update_refs):
        g = (me + ahead) % GROUPS
        for r in range(CAPACITY):
            update_ref[r] = buf[g * CAPACITY + r].reshape(BLOCK, 4 * HD)[:, 3 * HD :]


def pick(shards, slots, ingested):
    count = GROUPS * CAPACITY
    update = jax.ShapeDtypeStruct((CAPACITY, BLOCK, HD), jnp.bfloat16)
    return pl.pallas_call(
        pick_kernel,
        out_shape=[jax.ShapeDtypeStruct((count, BLOCK, 3 * HD), jnp.bfloat16)] + [update] * GROUPS,
        in_specs=[SMEM, SMEM, ANY],
        out_specs=[VMEM] * (1 + GROUPS),
        scratch_shapes=[
            pltpu.VMEM((count, BLOCK, 4, HD), jnp.bfloat16),
            pltpu.SemaphoreType.DMA((count,)),
        ],
        compiler_params=params(56),
    )(shards, slots, ingested)


def block_sources(shard_ref):
    me = lax.axis_index("batch")
    shards = [shard_ref[me, k] for k in range(PER_OWNER)]
    for k in range(PER_OWNER):
        rank = jnp.int32(0)
        for earlier in range(k):
            rank = rank + (shards[earlier] == shards[k]).astype(jnp.int32)
        yield slice(k * BLOCK, (k + 1) * BLOCK), shards[k], rank


def order_kernel(shard_ref, in_ref, *refs):
    unit_ref, query_ref = refs[len(refs) // 2 - 1 : len(refs) // 2 + 1]
    for rows, shard, rank in block_sources(shard_ref):
        at = shard * CAPACITY + rank
        query_ref[rows, :] = in_ref[at, :, :HD]
        unit_ref[rows, :] = in_ref[at, :, HD:]


def in_order(shards, blocks, later):
    return pl.pallas_call(
        order_kernel,
        out_shape=[
            jax.ShapeDtypeStruct((ROWS, 2 * HD), jnp.bfloat16),
            jax.ShapeDtypeStruct((ROWS, HD), jnp.bfloat16),
        ]
        + [jax.ShapeDtypeStruct(x.shape, x.dtype) for x in later],
        in_specs=[SMEM, VMEM] + [ANY] * len(later),
        out_specs=[VMEM] * 2 + [ANY] * len(later),
        input_output_aliases={2 + i: 2 + i for i in range(len(later))},
        compiler_params=params(),
    )(shards, blocks, *later)


def unit_owner(stream, step):
    me = lax.axis_index("ctx")
    plane, row = me // PLANE, me % PLANE
    wrapped = plane * PLANE + (row + step) % PLANE if step < 4 else -1
    return jnp.where((row + stream) % 2 == 1, me - step, wrapped)


def history_ends(hist_ref):
    ends, total = [], jnp.int32(0)
    for u in range(4):
        total = total + hist_ref[0, u]
        ends.append(total)
    return ends


def start_of(ends, pos):
    start = jnp.zeros_like(pos)
    for e in ends:
        start = jnp.where(pos >= e, jnp.maximum(start, e), start)
    return start


def silu_of_dot(q, k):
    s = lax.dot_general(q, k, (((1,), (1,)), ((), ())), preferred_element_type=jnp.float32)
    h = s * HALF_SCALE
    return h + h * jnp.tanh(h)


def add_units(ends, q_base, q_ref, units, acc_ref):
    def row_tile(t, _):
        rows = pl.ds(pl.multiple_of(t * TILE, TILE), TILE)
        first = q_base + t * TILE
        last = first + TILE - 1
        low, high = start_of(ends, first), start_of(ends, last)
        pos = first + lax.broadcasted_iota(jnp.int32, (TILE, 1), 0)
        start = start_of(ends, pos)
        for owner, unit in units:
            base = owner * ROWS
            some = (base <= last) & (base + ROWS - 1 >= low)
            whole = (base + ROWS - 1 <= first) & (base >= high)

            @pl.when(whole)
            def _():
                w = silu_of_dot(q_ref[rows, :], unit[:, :HD]).astype(jnp.bfloat16)
                acc_ref[rows, :] += jnp.dot(w, unit[:, HD:], preferred_element_type=jnp.float32)

            @pl.when(some & jnp.logical_not(whole))
            def _():
                for part in range(ROWS // TILE):
                    k_first = base + part * TILE
                    keys = slice(part * TILE, (part + 1) * TILE)

                    @pl.when((k_first <= last) & (k_first + TILE - 1 >= low))
                    def _():
                        key = k_first + lax.broadcasted_iota(jnp.int32, (TILE, TILE), 1)
                        seen = (key <= pos) & (key >= start)
                        w = silu_of_dot(q_ref[rows, :], unit[keys, :HD])
                        w = jnp.where(seen, w, 0.0).astype(jnp.bfloat16)
                        acc_ref[rows, :] += jnp.dot(
                            w, unit[keys, HD:], preferred_element_type=jnp.float32
                        )

        return 0

    lax.fori_loop(0, ROWS // TILE, row_tile, 0)


def attend_kernel(names, first, hist_ref, q_ref, *refs):
    units, refs = refs[: len(names)], refs[len(names) :]
    acc_ref = refs[-1]
    if first:
        acc_ref[...] = jnp.zeros_like(acc_ref)
    else:
        acc_ref[...] = refs[0][...]
    me = lax.axis_index("ctx")
    ends = history_ends(hist_ref)
    owners = [unit_owner(*name) for name in names]
    add_units(ends, me * ROWS, q_ref, list(zip(owners, units)), acc_ref)


def estimate(units):
    return pl.CostEstimate(
        flops=WEIGHT * 4 * ROWS * ROWS * HD * units,
        bytes_accessed=1 << 20,
        transcendentals=ROWS * ROWS * units,
    )


def attend(hist, q, units, names, acc=None):
    first = acc is None
    return pl.pallas_call(
        functools.partial(attend_kernel, names, first),
        out_shape=jax.ShapeDtypeStruct((ROWS, HD), jnp.float32),
        in_specs=[SMEM] + [VMEM] * (1 + len(units) + (0 if first else 1)),
        out_specs=VMEM,
        cost_estimate=estimate(len(units)),
        compiler_params=params(),
    )(hist, q, *units, *(() if first else (acc,)))


def lent_kernel(names, first, final, hist_ref, q_ref, *refs):
    units, refs = refs[: len(names)], refs[len(names) :]
    acc_ref = refs[-1]
    if first:
        acc_ref[...] = jnp.zeros_like(acc_ref)
    else:
        acc_ref[...] = refs[0][...]
    me = lax.axis_index("ctx")

    @pl.when(me < PLANE)
    def _():
        ends = history_ends(hist_ref)
        owners = [unit_owner(*name) for name in names]
        add_units(ends, (me + PLANE) * ROWS, q_ref, list(zip(owners, units)), acc_ref)

    if final:
        refs[-2][...] = acc_ref[...].astype(jnp.bfloat16)


def attend_lent(hist, q, units, names, acc=None, final=False):
    first = acc is None
    return pl.pallas_call(
        functools.partial(lent_kernel, names, first, final),
        out_shape=jax.ShapeDtypeStruct((ROWS, HD), jnp.bfloat16 if final else jnp.float32),
        in_specs=[SMEM] + [VMEM] * (1 + len(units) + (0 if first else 1)),
        out_specs=VMEM,
        scratch_shapes=[pltpu.VMEM((ROWS, HD), jnp.float32)] if final else [],
        cost_estimate=estimate(len(units)),
        compiler_params=params(),
    )(hist, q, *units, *(() if first else (acc,)))


def last_kernel(names, hist_ref, shard_ref, q_ref, *refs):
    units = refs[: len(names)]
    acc_in, lent_ref, *update_refs, out_ref, acc_ref = refs[len(names) :]
    me = lax.axis_index("ctx")
    acc_ref[...] = acc_in[...]

    @pl.when(me >= PLANE)
    def _():
        acc_ref[...] += lent_ref[...].astype(jnp.float32)

    ends = history_ends(hist_ref)
    owners = [unit_owner(*name) for name in names]
    add_units(ends, me * ROWS, q_ref, list(zip(owners, units)), acc_ref)
    group = lax.axis_index("batch")
    for rows, shard, rank in block_sources(shard_ref):
        a = acc_ref[rows, :]
        mean = jnp.mean(a * a, axis=-1, keepdims=True)
        normed = a * lax.rsqrt(mean + 1e-6)
        behind = (group + GROUPS - shard) % GROUPS
        update = update_refs[0][rank]
        for d in range(1, GROUPS):
            update = jnp.where(behind == d, update_refs[d][rank], update)
        out_ref[rows, :] = (normed * update.astype(jnp.float32)).astype(jnp.bfloat16)


def attend_last(hist, shards, q, units, names, acc, lent, updates):
    return pl.pallas_call(
        functools.partial(last_kernel, names),
        out_shape=jax.ShapeDtypeStruct((ROWS, HD), jnp.bfloat16),
        in_specs=[SMEM, SMEM] + [VMEM] * (3 + len(units) + len(updates)),
        out_specs=VMEM,
        scratch_shapes=[pltpu.VMEM((ROWS, HD), jnp.float32)],
        cost_estimate=estimate(len(units)),
        compiler_params=params(),
    )(hist, shards, q, *units, acc, lent, *updates)


def near_heads(head):
    chip, core = head // 2, head % 2
    even = chip + 1 - 2 * (chip % 2)
    odd = (chip + 3 + 2 * (chip % 2)) % 4
    return head, even * 2 + core, odd * 2 + core, (head + 4) % HEADS


def project_kernel(rows_ref, mine_ref, theirs_ref, out_ref):
    me = lax.axis_index("head")
    total = 0.0
    for head, w_ref in ((me, mine_ref), (me + 1 - 2 * (me % 2), theirs_ref)):
        rows = jnp.concatenate([rows_ref[h] for h in near_heads(head)], axis=1)
        total = total + jnp.dot(rows, w_ref[...], preferred_element_type=jnp.float32)
    mixed = total.astype(jnp.bfloat16)
    for h in range(HEADS):
        out_ref[h] = mixed[:, h * HD : (h + 1) * HD]


def project(rows, mine, theirs):
    return pl.pallas_call(
        project_kernel,
        out_shape=jax.ShapeDtypeStruct((HEADS, CHUNK, HD), jnp.bfloat16),
        in_specs=[VMEM] * 3,
        out_specs=VMEM,
        compiler_params=params(),
    )(rows, mine, theirs)


CORE = [(h, h ^ 1) for h in range(HEADS)]
X_EVEN = [(h, near_heads(h)[1]) for h in range(HEADS)]
X_ODD = [(h, near_heads(h)[2]) for h in range(HEADS)]
UP = [(i, i + 1) for i in range(CTXS - 1)]
DOWN = [(i, i // PLANE * PLANE + (i - 1) % PLANE) for i in range(CTXS)]
LEND = [(i + PLANE, i) for i in range(PLANE)]
RETURN = [(i, i + PLANE) for i in range(PLANE)]


def stream_pairs(stream, step):
    ups = [(i, j) for i, j in UP if i % 2 == stream]
    downs = [(i, j) for i, j in DOWN if i % 2 != stream]
    return ups + (downs if step < 4 else [])


def gather_w(w):
    cross = functools.partial(lax.ppermute, axis_name="head")
    half = HD // 2
    even, odd = cross(w, perm=X_EVEN), cross(w, perm=X_ODD)
    far = [cross(odd[:half], perm=X_EVEN), cross(even[half:], perm=X_ODD)]
    mine = jnp.concatenate([w, even, odd, *far])
    return mine, cross(mine, perm=CORE)


def body(ingest, src_shard, src_slot, hist_len, w_out):
    ingested, shards, slots = ingest[0, 0], src_shard[0], src_slot[0]
    move = functools.partial(lax.ppermute, axis_name="ctx")

    def to_all(x):
        return lax.all_to_all(x, "head", 0, 0, tiled=True)

    def step_on(last, step):
        return [move(last[1 - stream], perm=stream_pairs(stream, step)) for stream in range(2)]

    names = [((0, 0),)] + [((0, step), (1, step)) for step in range(1, 5)]
    blocks, *updates = pick(shards, slots, ingested)
    w_late, blocks = lax.optimization_barrier((w_out, blocks))
    arrived = lax.all_to_all(blocks, "batch", split_axis=0, concat_axis=0, tiled=True)
    mine, theirs = gather_w(w_late)
    mine, arrived = lax.optimization_barrier((mine, arrived))
    own, q, *sent = in_order(shards, arrived, updates[1:])
    for ahead in range(1, GROUPS):
        pairs = [(i, (i + ahead) % GROUPS) for i in range(GROUPS)]
        updates[ahead] = lax.ppermute(sent[ahead - 1], "batch", pairs)
    first = step_on([own, own], 1)
    second = step_on(first, 2)
    third = step_on(second, 3)
    fourth = step_on(third, 4)
    lent_q = move(q, perm=LEND)
    acc = attend(hist_len, q, (own,), names[0])
    acc = attend(hist_len, q, first, names[1], acc)
    lent = attend_lent(hist_len, lent_q, (own, *first), names[0] + names[1])
    acc = attend(hist_len, q, second, names[2], acc)
    lent = attend_lent(hist_len, lent_q, second, names[2], lent)
    lent = attend_lent(hist_len, lent_q, third, names[3], lent, final=True)
    lent = move(lent, perm=RETURN)
    acc = attend(hist_len, q, third, names[3], acc)
    gated = attend_last(hist_len, shards, q, fourth, names[4], acc, lent, updates)
    rows = to_all(gated.reshape(HEADS, CHUNK, HD))
    mixed = to_all(project(rows, mine, theirs))
    return mixed.reshape(1, ROWS, HD)


def solution(mesh):
    in_specs = (
        P("ctx", "batch", None, None, None, "head"),
        P("ctx", None, None),
        P("ctx", None, None),
        P("batch", None),
        P("head", None),
    )
    out_specs = P("batch", "ctx", "head")
    return jax.shard_map(body, mesh=mesh, in_specs=in_specs, out_specs=out_specs, check_vma=False)
```

```python
import functools
import math

import jax
import jax.numpy as jnp
from jax import lax
from jax.experimental import pallas as pl
from jax.experimental.pallas import tpu as pltpu
from jax.sharding import PartitionSpec as P

HD = 128
BLOCK = 128
PER_OWNER = 6
CAPACITY = 3
GROUPS = 4
CTXS = 16
PLANE = 8
HEADS = 8
ROWS = BLOCK * PER_OWNER
CHUNK = ROWS // HEADS
TILE = 256
WEIGHT = 8
HALF_SCALE = 0.5 / math.sqrt(HD)
VMEM = pl.BlockSpec(memory_space=pltpu.VMEM)
SMEM = pl.BlockSpec(memory_space=pltpu.SMEM)
ANY = pl.BlockSpec(memory_space=pl.ANY)


def params(mib=16):
    return pltpu.CompilerParams(vmem_limit_bytes=mib * 1024 * 1024)


def pick_kernel(shard_ref, slot_ref, ingest_ref, out_ref, buf, sems):
    me = lax.axis_index("batch")
    copies = []
    for g in range(GROUPS):
        seen = jnp.int32(0)
        slots = [jnp.int32(0)] * CAPACITY
        for k in range(PER_OWNER):
            hit = shard_ref[g, k] == me
            slot = slot_ref[g, k]
            for r in range(CAPACITY):
                slots[r] = jnp.where(hit & (seen == r), slot, slots[r])
            seen = seen + hit.astype(jnp.int32)
        for r in range(CAPACITY):
            at = g * CAPACITY + r
            copy = pltpu.make_async_copy(ingest_ref.at[slots[r]], buf.at[at], sems.at[at])
            copy.start()
            copies.append(copy)
    for at, copy in enumerate(copies):
        copy.wait()
        out_ref[at] = buf[at].reshape(BLOCK, 4 * HD)


def pick(shards, slots, ingested):
    count = GROUPS * CAPACITY
    return pl.pallas_call(
        pick_kernel,
        out_shape=jax.ShapeDtypeStruct((count, BLOCK, 4 * HD), jnp.bfloat16),
        in_specs=[SMEM, SMEM, ANY],
        out_specs=VMEM,
        scratch_shapes=[
            pltpu.VMEM((count, BLOCK, 4, HD), jnp.bfloat16),
            pltpu.SemaphoreType.DMA((count,)),
        ],
        compiler_params=params(56),
    )(shards, slots, ingested)


def block_places(shard_ref):
    me = lax.axis_index("batch")
    shards = [shard_ref[me, k] for k in range(PER_OWNER)]
    for k in range(PER_OWNER):
        rank = jnp.int32(0)
        for earlier in range(k):
            rank = rank + (shards[earlier] == shards[k]).astype(jnp.int32)
        yield slice(k * BLOCK, (k + 1) * BLOCK), shards[k] * CAPACITY + rank


def order_kernel(shard_ref, in_ref, unit_ref, query_ref, update_ref):
    for rows, at in block_places(shard_ref):
        query_ref[rows, :] = in_ref[at, :, :HD]
        unit_ref[rows, :] = in_ref[at, :, HD : 3 * HD]
        update_ref[rows, :] = in_ref[at, :, 3 * HD :]


def in_order(shards, blocks):
    shape = jax.ShapeDtypeStruct((ROWS, HD), jnp.bfloat16)
    return pl.pallas_call(
        order_kernel,
        out_shape=[jax.ShapeDtypeStruct((ROWS, 2 * HD), jnp.bfloat16), shape, shape],
        in_specs=[SMEM, VMEM],
        out_specs=[VMEM] * 3,
        compiler_params=params(),
    )(shards, blocks)


def unit_owner(stream, step):
    me = lax.axis_index("ctx")
    if stream == "up":
        return me - step
    return me // PLANE * PLANE + (me % PLANE + step) % PLANE


def history_ends(hist_ref):
    ends, total = [], jnp.int32(0)
    for u in range(4):
        total = total + hist_ref[0, u]
        ends.append(total)
    return ends


def start_of(ends, pos):
    start = jnp.zeros_like(pos)
    for e in ends:
        start = jnp.where(pos >= e, jnp.maximum(start, e), start)
    return start


def silu_of_dot(q, k):
    s = lax.dot_general(q, k, (((1,), (1,)), ((), ())), preferred_element_type=jnp.float32)
    h = s * HALF_SCALE
    return h + h * jnp.tanh(h)


def add_units(ends, q_base, q_ref, units, acc_ref):
    def row_tile(t, _):
        rows = pl.ds(pl.multiple_of(t * TILE, TILE), TILE)
        first = q_base + t * TILE
        last = first + TILE - 1
        low, high = start_of(ends, first), start_of(ends, last)
        pos = first + lax.broadcasted_iota(jnp.int32, (TILE, 1), 0)
        start = start_of(ends, pos)
        for owner, unit in units:
            base = owner * ROWS
            some = (base <= last) & (base + ROWS - 1 >= low)
            whole = (base + ROWS - 1 <= first) & (base >= high)

            @pl.when(whole)
            def _():
                w = silu_of_dot(q_ref[rows, :], unit[:, :HD]).astype(jnp.bfloat16)
                acc_ref[rows, :] += jnp.dot(w, unit[:, HD:], preferred_element_type=jnp.float32)

            @pl.when(some & jnp.logical_not(whole))
            def _():
                for part in range(ROWS // TILE):
                    k_first = base + part * TILE
                    keys = slice(part * TILE, (part + 1) * TILE)

                    @pl.when((k_first <= last) & (k_first + TILE - 1 >= low))
                    def _():
                        key = k_first + lax.broadcasted_iota(jnp.int32, (TILE, TILE), 1)
                        seen = (key <= pos) & (key >= start)
                        w = silu_of_dot(q_ref[rows, :], unit[keys, :HD])
                        w = jnp.where(seen, w, 0.0).astype(jnp.bfloat16)
                        acc_ref[rows, :] += jnp.dot(
                            w, unit[keys, HD:], preferred_element_type=jnp.float32
                        )

        return 0

    lax.fori_loop(0, ROWS // TILE, row_tile, 0)


def attend_kernel(names, first, hist_ref, q_ref, *refs):
    units, refs = refs[: len(names)], refs[len(names) :]
    acc_ref = refs[-1]
    if first:
        acc_ref[...] = jnp.zeros_like(acc_ref)
    else:
        acc_ref[...] = refs[0][...]
    me = lax.axis_index("ctx")
    ends = history_ends(hist_ref)
    owners = [unit_owner(*name) for name in names]
    add_units(ends, me * ROWS, q_ref, list(zip(owners, units)), acc_ref)


def estimate(units):
    return pl.CostEstimate(
        flops=WEIGHT * 4 * ROWS * ROWS * HD * units,
        bytes_accessed=1 << 20,
        transcendentals=ROWS * ROWS * units,
    )


def attend(hist, q, units, names, acc=None):
    first = acc is None
    return pl.pallas_call(
        functools.partial(attend_kernel, names, first),
        out_shape=jax.ShapeDtypeStruct((ROWS, HD), jnp.float32),
        in_specs=[SMEM] + [VMEM] * (1 + len(units) + (0 if first else 1)),
        out_specs=VMEM,
        cost_estimate=estimate(len(units)),
        compiler_params=params(),
    )(hist, q, *units, *(() if first else (acc,)))


def lent_kernel(names, first, final, hist_ref, q_ref, *refs):
    units, refs = refs[: len(names)], refs[len(names) :]
    acc_ref = refs[-1]
    if first:
        acc_ref[...] = jnp.zeros_like(acc_ref)
    else:
        acc_ref[...] = refs[0][...]
    me = lax.axis_index("ctx")

    @pl.when(me < PLANE)
    def _():
        ends = history_ends(hist_ref)
        owners = [unit_owner(*name) for name in names]
        add_units(ends, (me + PLANE) * ROWS, q_ref, list(zip(owners, units)), acc_ref)

    if final:
        refs[-2][...] = acc_ref[...].astype(jnp.bfloat16)


def attend_lent(hist, q, units, names, acc=None, final=False):
    first = acc is None
    return pl.pallas_call(
        functools.partial(lent_kernel, names, first, final),
        out_shape=jax.ShapeDtypeStruct((ROWS, HD), jnp.bfloat16 if final else jnp.float32),
        in_specs=[SMEM] + [VMEM] * (1 + len(units) + (0 if first else 1)),
        out_specs=VMEM,
        scratch_shapes=[pltpu.VMEM((ROWS, HD), jnp.float32)] if final else [],
        cost_estimate=estimate(len(units)),
        compiler_params=params(),
    )(hist, q, *units, *(() if first else (acc,)))


def last_kernel(names, hist_ref, q_ref, *refs):
    units = refs[: len(names)]
    acc_in, lent_ref, update_ref, out_ref, acc_ref = refs[len(names) :]
    me = lax.axis_index("ctx")
    acc_ref[...] = acc_in[...]

    @pl.when(me >= PLANE)
    def _():
        acc_ref[...] += lent_ref[...].astype(jnp.float32)

    ends = history_ends(hist_ref)
    owners = [unit_owner(*name) for name in names]
    add_units(ends, me * ROWS, q_ref, list(zip(owners, units)), acc_ref)
    a = acc_ref[...]
    mean = jnp.mean(a * a, axis=-1, keepdims=True)
    normed = a * lax.rsqrt(mean + 1e-6)
    out_ref[...] = (normed * update_ref[...].astype(jnp.float32)).astype(jnp.bfloat16)


def attend_last(hist, q, units, names, acc, lent, update):
    return pl.pallas_call(
        functools.partial(last_kernel, names),
        out_shape=jax.ShapeDtypeStruct((ROWS, HD), jnp.bfloat16),
        in_specs=[SMEM] + [VMEM] * (4 + len(units)),
        out_specs=VMEM,
        scratch_shapes=[pltpu.VMEM((ROWS, HD), jnp.float32)],
        cost_estimate=estimate(len(units)),
        compiler_params=params(),
    )(hist, q, *units, acc, lent, update)


def near_heads(head):
    chip, core = head // 2, head % 2
    even = chip + 1 - 2 * (chip % 2)
    odd = (chip + 3 + 2 * (chip % 2)) % 4
    return head, even * 2 + core, odd * 2 + core, (head + 4) % HEADS


def project_kernel(rows_ref, mine_ref, theirs_ref, out_ref):
    me = lax.axis_index("head")
    total = 0.0
    for head, w_ref in ((me, mine_ref), (me + 1 - 2 * (me % 2), theirs_ref)):
        rows = jnp.concatenate([rows_ref[h] for h in near_heads(head)], axis=1)
        total = total + jnp.dot(rows, w_ref[...], preferred_element_type=jnp.float32)
    mixed = total.astype(jnp.bfloat16)
    for h in range(HEADS):
        out_ref[h] = mixed[:, h * HD : (h + 1) * HD]


def project(rows, mine, theirs):
    return pl.pallas_call(
        project_kernel,
        out_shape=jax.ShapeDtypeStruct((HEADS, CHUNK, HD), jnp.bfloat16),
        in_specs=[VMEM] * 3,
        out_specs=VMEM,
        compiler_params=params(),
    )(rows, mine, theirs)


CORE = [(h, h ^ 1) for h in range(HEADS)]
X_EVEN = [(h, near_heads(h)[1]) for h in range(HEADS)]
X_ODD = [(h, near_heads(h)[2]) for h in range(HEADS)]
UP = [(i, i + 1) for i in range(CTXS - 1)]
DOWN = [(i, i // PLANE * PLANE + (i - 1) % PLANE) for i in range(CTXS)]
LEND = [(i + PLANE, i) for i in range(PLANE)]
RETURN = [(i, i + PLANE) for i in range(PLANE)]


def gather_w(w):
    cross = functools.partial(lax.ppermute, axis_name="head")
    half = HD // 2
    even, odd = cross(w, perm=X_EVEN), cross(w, perm=X_ODD)
    far = [cross(odd[:half], perm=X_EVEN), cross(even[half:], perm=X_ODD)]
    mine = jnp.concatenate([w, even, odd, *far])
    return mine, cross(mine, perm=CORE)


def body(ingest, src_shard, src_slot, hist_len, w_out):
    ingested, shards, slots = ingest[0, 0], src_shard[0], src_slot[0]
    move = functools.partial(lax.ppermute, axis_name="ctx")

    def to_all(x):
        return lax.all_to_all(x, "head", 0, 0, tiled=True)

    blocks = pick(shards, slots, ingested)
    w_late, blocks = lax.optimization_barrier((w_out, blocks))
    arrived = lax.all_to_all(blocks, "batch", split_axis=0, concat_axis=0, tiled=True)
    mine, theirs = gather_w(w_late)
    mine, theirs, arrived = lax.optimization_barrier((mine, theirs, arrived))
    own, q, update = in_order(shards, arrived)
    up, down = [own], [own]
    for step in range(4):
        up.append(move(up[-1], perm=UP))
        if step < 3:
            down.append(move(down[-1], perm=DOWN))
    lent_q = move(q, perm=LEND)
    acc = attend(hist_len, q, (own,), (("up", 0),))
    acc = attend(hist_len, q, (up[1], down[1]), (("up", 1), ("down", 1)), acc)
    lent = attend_lent(hist_len, lent_q, (own, down[1]), (("down", 0), ("down", 1)))
    acc = attend(hist_len, q, (up[2], down[2]), (("up", 2), ("down", 2)), acc)
    lent = attend_lent(
        hist_len, lent_q, (down[2], down[3]), (("down", 2), ("down", 3)), lent, final=True
    )
    lent = move(lent, perm=RETURN)
    acc = attend(hist_len, q, (up[3], down[3]), (("up", 3), ("down", 3)), acc)
    gated = attend_last(hist_len, q, (up[4],), (("up", 4),), acc, lent, update)
    rows = to_all(gated.reshape(HEADS, CHUNK, HD))
    mixed = to_all(project(rows, mine, theirs))
    return mixed.reshape(1, ROWS, HD)


def solution(mesh):
    in_specs = (
        P("ctx", "batch", None, None, None, "head"),
        P("ctx", None, None),
        P("ctx", None, None),
        P("batch", None),
        P("head", None),
    )
    out_specs = P("batch", "ctx", "head")
    return jax.shard_map(body, mesh=mesh, in_specs=in_specs, out_specs=out_specs, check_vma=False)
```

```python
import functools
import math

import jax
import jax.numpy as jnp
from jax import lax
from jax.experimental import pallas as pl
from jax.experimental.pallas import tpu as pltpu
from jax.sharding import PartitionSpec as P

HD = 128
BLOCK = 128
PER_OWNER = 6
CAPACITY = 3
GROUPS = 4
CTXS = 16
PLANE = 8
HEADS = 8
ROWS = BLOCK * PER_OWNER
CHUNK = ROWS // HEADS
TILE = 256
WEIGHT = 8
HALF_SCALE = 0.5 / math.sqrt(HD)
VMEM = pl.BlockSpec(memory_space=pltpu.VMEM)
SMEM = pl.BlockSpec(memory_space=pltpu.SMEM)
ANY = pl.BlockSpec(memory_space=pl.ANY)


def params(mib=16):
    return pltpu.CompilerParams(vmem_limit_bytes=mib * 1024 * 1024)


def pick_kernel(shard_ref, slot_ref, ingest_ref, out_ref, buf, sems):
    me = lax.axis_index("batch")
    copies = []
    for g in range(GROUPS):
        seen = jnp.int32(0)
        slots = [jnp.int32(0)] * CAPACITY
        for k in range(PER_OWNER):
            hit = shard_ref[g, k] == me
            slot = slot_ref[g, k]
            for r in range(CAPACITY):
                slots[r] = jnp.where(hit & (seen == r), slot, slots[r])
            seen = seen + hit.astype(jnp.int32)
        for r in range(CAPACITY):
            at = g * CAPACITY + r
            copy = pltpu.make_async_copy(ingest_ref.at[slots[r]], buf.at[at], sems.at[at])
            copy.start()
            copies.append(copy)
    for at, copy in enumerate(copies):
        copy.wait()
        out_ref[at] = buf[at].reshape(BLOCK, 4 * HD)


def pick(shards, slots, ingested):
    count = GROUPS * CAPACITY
    return pl.pallas_call(
        pick_kernel,
        out_shape=jax.ShapeDtypeStruct((count, BLOCK, 4 * HD), jnp.bfloat16),
        in_specs=[SMEM, SMEM, ANY],
        out_specs=VMEM,
        scratch_shapes=[
            pltpu.VMEM((count, BLOCK, 4, HD), jnp.bfloat16),
            pltpu.SemaphoreType.DMA((count,)),
        ],
        compiler_params=params(56),
    )(shards, slots, ingested)


def block_places(shard_ref):
    me = lax.axis_index("batch")
    shards = [shard_ref[me, k] for k in range(PER_OWNER)]
    for k in range(PER_OWNER):
        rank = jnp.int32(0)
        for earlier in range(k):
            rank = rank + (shards[earlier] == shards[k]).astype(jnp.int32)
        yield slice(k * BLOCK, (k + 1) * BLOCK), shards[k] * CAPACITY + rank


def order_kernel(shard_ref, in_ref, unit_ref, query_ref, update_ref):
    for rows, at in block_places(shard_ref):
        query_ref[rows, :] = in_ref[at, :, :HD]
        unit_ref[rows, :] = in_ref[at, :, HD : 3 * HD]
        update_ref[rows, :] = in_ref[at, :, 3 * HD :]


def in_order(shards, blocks):
    shape = jax.ShapeDtypeStruct((ROWS, HD), jnp.bfloat16)
    return pl.pallas_call(
        order_kernel,
        out_shape=[jax.ShapeDtypeStruct((ROWS, 2 * HD), jnp.bfloat16), shape, shape],
        in_specs=[SMEM, VMEM],
        out_specs=[VMEM] * 3,
        compiler_params=params(),
    )(shards, blocks)


def unit_owner(stream, step):
    me = lax.axis_index("ctx")
    if step == 4:
        return me - step
    ahead = step if stream == "down" else PLANE - step
    return me // PLANE * PLANE + (me % PLANE + ahead) % PLANE


def history_ends(hist_ref):
    ends, total = [], jnp.int32(0)
    for u in range(4):
        total = total + hist_ref[0, u]
        ends.append(total)
    return ends


def start_of(ends, pos):
    start = jnp.zeros_like(pos)
    for e in ends:
        start = jnp.where(pos >= e, jnp.maximum(start, e), start)
    return start


def silu_of_dot(q, k):
    s = lax.dot_general(q, k, (((1,), (1,)), ((), ())), preferred_element_type=jnp.float32)
    h = s * HALF_SCALE
    return h + h * jnp.tanh(h)


def add_units(ends, q_base, q_ref, units, acc_ref):
    def row_tile(t, _):
        rows = pl.ds(pl.multiple_of(t * TILE, TILE), TILE)
        first = q_base + t * TILE
        last = first + TILE - 1
        low, high = start_of(ends, first), start_of(ends, last)
        pos = first + lax.broadcasted_iota(jnp.int32, (TILE, 1), 0)
        start = start_of(ends, pos)
        for owner, unit in units:
            base = owner * ROWS
            some = (base <= last) & (base + ROWS - 1 >= low)
            whole = (base + ROWS - 1 <= first) & (base >= high)

            @pl.when(whole)
            def _():
                w = silu_of_dot(q_ref[rows, :], unit[:, :HD]).astype(jnp.bfloat16)
                acc_ref[rows, :] += jnp.dot(w, unit[:, HD:], preferred_element_type=jnp.float32)

            @pl.when(some & jnp.logical_not(whole))
            def _():
                for part in range(ROWS // TILE):
                    k_first = base + part * TILE
                    keys = slice(part * TILE, (part + 1) * TILE)

                    @pl.when((k_first <= last) & (k_first + TILE - 1 >= low))
                    def _():
                        key = k_first + lax.broadcasted_iota(jnp.int32, (TILE, TILE), 1)
                        seen = (key <= pos) & (key >= start)
                        w = silu_of_dot(q_ref[rows, :], unit[keys, :HD])
                        w = jnp.where(seen, w, 0.0).astype(jnp.bfloat16)
                        acc_ref[rows, :] += jnp.dot(
                            w, unit[keys, HD:], preferred_element_type=jnp.float32
                        )

        return 0

    lax.fori_loop(0, ROWS // TILE, row_tile, 0)


def attend_kernel(names, first, hist_ref, q_ref, *refs):
    units, refs = refs[: len(names)], refs[len(names) :]
    acc_ref = refs[-1]
    if first:
        acc_ref[...] = jnp.zeros_like(acc_ref)
    else:
        acc_ref[...] = refs[0][...]
    me = lax.axis_index("ctx")
    ends = history_ends(hist_ref)
    owners = [unit_owner(*name) for name in names]
    add_units(ends, me * ROWS, q_ref, list(zip(owners, units)), acc_ref)


def estimate(units):
    return pl.CostEstimate(
        flops=WEIGHT * 4 * ROWS * ROWS * HD * units,
        bytes_accessed=1 << 20,
        transcendentals=ROWS * ROWS * units,
    )


def attend(hist, q, units, names, acc=None):
    first = acc is None
    return pl.pallas_call(
        functools.partial(attend_kernel, names, first),
        out_shape=jax.ShapeDtypeStruct((ROWS, HD), jnp.float32),
        in_specs=[SMEM] + [VMEM] * (1 + len(units) + (0 if first else 1)),
        out_specs=VMEM,
        cost_estimate=estimate(len(units)),
        compiler_params=params(),
    )(hist, q, *units, *(() if first else (acc,)))


def lent_kernel(names, first, final, hist_ref, q_ref, *refs):
    units, refs = refs[: len(names)], refs[len(names) :]
    acc_ref = refs[-1]
    if first:
        acc_ref[...] = jnp.zeros_like(acc_ref)
    else:
        acc_ref[...] = refs[0][...]
    me = lax.axis_index("ctx")

    @pl.when(me < PLANE)
    def _():
        ends = history_ends(hist_ref)
        owners = [unit_owner(*name) for name in names]
        add_units(ends, (me + PLANE) * ROWS, q_ref, list(zip(owners, units)), acc_ref)

    if final:
        refs[-2][...] = acc_ref[...].astype(jnp.bfloat16)


def attend_lent(hist, q, units, names, acc=None, final=False):
    first = acc is None
    return pl.pallas_call(
        functools.partial(lent_kernel, names, first, final),
        out_shape=jax.ShapeDtypeStruct((ROWS, HD), jnp.bfloat16 if final else jnp.float32),
        in_specs=[SMEM] + [VMEM] * (1 + len(units) + (0 if first else 1)),
        out_specs=VMEM,
        scratch_shapes=[pltpu.VMEM((ROWS, HD), jnp.float32)] if final else [],
        cost_estimate=estimate(len(units)),
        compiler_params=params(),
    )(hist, q, *units, *(() if first else (acc,)))


def last_kernel(names, hist_ref, q_ref, *refs):
    units = refs[: len(names)]
    acc_in, lent_ref, update_ref, out_ref, acc_ref = refs[len(names) :]
    me = lax.axis_index("ctx")
    acc_ref[...] = acc_in[...]

    @pl.when(me >= PLANE)
    def _():
        acc_ref[...] += lent_ref[...].astype(jnp.float32)

    ends = history_ends(hist_ref)
    owners = [unit_owner(*name) for name in names]
    add_units(ends, me * ROWS, q_ref, list(zip(owners, units)), acc_ref)
    a = acc_ref[...]
    mean = jnp.mean(a * a, axis=-1, keepdims=True)
    normed = a * lax.rsqrt(mean + 1e-6)
    out_ref[...] = (normed * update_ref[...].astype(jnp.float32)).astype(jnp.bfloat16)


def attend_last(hist, q, units, names, acc, lent, update):
    return pl.pallas_call(
        functools.partial(last_kernel, names),
        out_shape=jax.ShapeDtypeStruct((ROWS, HD), jnp.bfloat16),
        in_specs=[SMEM] + [VMEM] * (4 + len(units)),
        out_specs=VMEM,
        scratch_shapes=[pltpu.VMEM((ROWS, HD), jnp.float32)],
        cost_estimate=estimate(len(units)),
        compiler_params=params(),
    )(hist, q, *units, acc, lent, update)


def near_heads(head):
    chip, core = head // 2, head % 2
    even = chip + 1 - 2 * (chip % 2)
    odd = (chip + 3 + 2 * (chip % 2)) % 4
    return head, even * 2 + core, odd * 2 + core, (head + 4) % HEADS


def project_kernel(rows_ref, mine_ref, theirs_ref, out_ref):
    me = lax.axis_index("head")
    total = 0.0
    for head, w_ref in ((me, mine_ref), (me + 1 - 2 * (me % 2), theirs_ref)):
        rows = jnp.concatenate([rows_ref[h] for h in near_heads(head)], axis=1)
        total = total + jnp.dot(rows, w_ref[...], preferred_element_type=jnp.float32)
    mixed = total.astype(jnp.bfloat16)
    for h in range(HEADS):
        out_ref[h] = mixed[:, h * HD : (h + 1) * HD]


def project(rows, mine, theirs):
    return pl.pallas_call(
        project_kernel,
        out_shape=jax.ShapeDtypeStruct((HEADS, CHUNK, HD), jnp.bfloat16),
        in_specs=[VMEM] * 3,
        out_specs=VMEM,
        compiler_params=params(),
    )(rows, mine, theirs)


CORE = [(h, h ^ 1) for h in range(HEADS)]
X_EVEN = [(h, near_heads(h)[1]) for h in range(HEADS)]
X_ODD = [(h, near_heads(h)[2]) for h in range(HEADS)]
UP = [(i, i // PLANE * PLANE + (i + 1) % PLANE) for i in range(CTXS)]
DOWN = [(j, i) for i, j in UP]
LAST_UP = [(i % PLANE if j % PLANE < 4 else i, j) for i, j in UP if j >= 4]
LEND = [(i + PLANE, i) for i in range(PLANE)]
RETURN = [(i, i + PLANE) for i in range(PLANE)]


def gather_w(w):
    cross = functools.partial(lax.ppermute, axis_name="head")
    half = HD // 2
    even, odd = cross(w, perm=X_EVEN), cross(w, perm=X_ODD)
    far = [cross(odd[:half], perm=X_EVEN), cross(even[half:], perm=X_ODD)]
    mine = jnp.concatenate([w, even, odd, *far])
    return mine, cross(mine, perm=CORE)


def body(ingest, src_shard, src_slot, hist_len, w_out):
    ingested, shards, slots = ingest[0, 0], src_shard[0], src_slot[0]
    move = functools.partial(lax.ppermute, axis_name="ctx")

    def to_all(x):
        return lax.all_to_all(x, "head", 0, 0, tiled=True)

    blocks = pick(shards, slots, ingested)
    w_late, blocks = lax.optimization_barrier((w_out, blocks))
    arrived = lax.all_to_all(blocks, "batch", split_axis=0, concat_axis=0, tiled=True)
    mine, theirs = gather_w(w_late)
    mine, theirs, arrived = lax.optimization_barrier((mine, theirs, arrived))
    own, q, update = in_order(shards, arrived)
    up, down = [own], [own]
    for step in range(3):
        up.append(move(up[-1], perm=UP))
        down.append(move(down[-1], perm=DOWN))
    up.append(move(up[-1], perm=LAST_UP))
    names = [(("up", step), ("down", step)) for step in range(4)]
    units = list(zip(up, down))
    lent_q = move(q, perm=LEND)
    acc = attend(hist_len, q, (own,), (("up", 0),))
    acc = attend(hist_len, q, units[1], names[1], acc)
    lent = attend_lent(hist_len, lent_q, (own, *units[1]), (("up", 0), *names[1]))
    acc = attend(hist_len, q, units[2], names[2], acc)
    lent = attend_lent(hist_len, lent_q, units[2], names[2], lent)
    lent = attend_lent(hist_len, lent_q, units[3], names[3], lent, final=True)
    lent = move(lent, perm=RETURN)
    acc = attend(hist_len, q, units[3], names[3], acc)
    gated = attend_last(hist_len, q, (up[4],), (("up", 4),), acc, lent, update)
    rows = to_all(gated.reshape(HEADS, CHUNK, HD))
    mixed = to_all(project(rows, mine, theirs))
    return mixed.reshape(1, ROWS, HD)


def solution(mesh):
    in_specs = (
        P("ctx", "batch", None, None, None, "head"),
        P("ctx", None, None),
        P("ctx", None, None),
        P("batch", None),
        P("head", None),
    )
    out_specs = P("batch", "ctx", "head")
    return jax.shard_map(body, mesh=mesh, in_specs=in_specs, out_specs=out_specs, check_vma=False)
```

```python
import functools
import math

import jax
import jax.numpy as jnp
from jax import lax
from jax.experimental import pallas as pl
from jax.experimental.pallas import tpu as pltpu
from jax.sharding import PartitionSpec as P

HD = 128
BLOCK = 128
PER_OWNER = 6
CAPACITY = 3
GROUPS = 4
CTXS = 16
PLANE = 8
HEADS = 8
ROWS = BLOCK * PER_OWNER
CHUNK = ROWS // HEADS
TILE = 256
WEIGHT = 8
HALF_SCALE = 0.5 / math.sqrt(HD)
VMEM = pl.BlockSpec(memory_space=pltpu.VMEM)
SMEM = pl.BlockSpec(memory_space=pltpu.SMEM)
ANY = pl.BlockSpec(memory_space=pl.ANY)


def params(mib=16):
    return pltpu.CompilerParams(vmem_limit_bytes=mib * 1024 * 1024)


def pick_kernel(shard_ref, slot_ref, ingest_ref, unit_ref, row_ref, buf, sems):
    me = lax.axis_index("batch")
    copies = []
    for g in range(GROUPS):
        seen = jnp.int32(0)
        slots = [jnp.int32(0)] * CAPACITY
        for k in range(PER_OWNER):
            hit = shard_ref[g, k] == me
            slot = slot_ref[g, k]
            for r in range(CAPACITY):
                slots[r] = jnp.where(hit & (seen == r), slot, slots[r])
            seen = seen + hit.astype(jnp.int32)
        for r in range(CAPACITY):
            at = g * CAPACITY + r
            copy = pltpu.make_async_copy(ingest_ref.at[slots[r]], buf.at[at], sems.at[at])
            copy.start()
            copies.append(copy)
    for at, copy in enumerate(copies):
        copy.wait()
        flat = buf[at].reshape(BLOCK, 4 * HD)
        unit_ref[at] = flat[:, HD : 3 * HD]
        row_ref[at, :, :HD] = flat[:, :HD]
        row_ref[at, :, HD:] = flat[:, 3 * HD :]


def pick(shards, slots, ingested):
    count = GROUPS * CAPACITY
    return pl.pallas_call(
        pick_kernel,
        out_shape=[jax.ShapeDtypeStruct((count, BLOCK, 2 * HD), jnp.bfloat16)] * 2,
        in_specs=[SMEM, SMEM, ANY],
        out_specs=[VMEM] * 2,
        scratch_shapes=[
            pltpu.VMEM((count, BLOCK, 4, HD), jnp.bfloat16),
            pltpu.SemaphoreType.DMA((count,)),
        ],
        compiler_params=params(56),
    )(shards, slots, ingested)


def block_places(shard_ref):
    me = lax.axis_index("batch")
    shards = [shard_ref[me, k] for k in range(PER_OWNER)]
    for k in range(PER_OWNER):
        rank = jnp.int32(0)
        for earlier in range(k):
            rank = rank + (shards[earlier] == shards[k]).astype(jnp.int32)
        yield slice(k * BLOCK, (k + 1) * BLOCK), shards[k] * CAPACITY + rank


def order_unit_kernel(shard_ref, in_ref, unit_ref):
    for rows, at in block_places(shard_ref):
        unit_ref[rows, :] = in_ref[at]


def order_unit(shards, blocks):
    return pl.pallas_call(
        order_unit_kernel,
        out_shape=jax.ShapeDtypeStruct((ROWS, 2 * HD), jnp.bfloat16),
        in_specs=[SMEM, VMEM],
        out_specs=VMEM,
        compiler_params=params(),
    )(shards, blocks)


def order_rows_kernel(shard_ref, in_ref, *refs):
    query_ref, update_ref = refs[-2:]
    for rows, at in block_places(shard_ref):
        query_ref[rows, :] = in_ref[at, :, :HD]
        update_ref[rows, :] = in_ref[at, :, HD:]


def order_rows(shards, blocks, earlier):
    return pl.pallas_call(
        order_rows_kernel,
        out_shape=[jax.ShapeDtypeStruct((ROWS, HD), jnp.bfloat16)] * 2,
        in_specs=[SMEM, VMEM] + [ANY] * len(earlier),
        out_specs=[VMEM] * 2,
        compiler_params=params(),
    )(shards, blocks, *earlier)


def unit_owner(stream, step):
    me = lax.axis_index("ctx")
    if stream == "up":
        return me - step
    return me // PLANE * PLANE + (me % PLANE + step) % PLANE


def history_ends(hist_ref):
    ends, total = [], jnp.int32(0)
    for u in range(4):
        total = total + hist_ref[0, u]
        ends.append(total)
    return ends


def start_of(ends, pos):
    start = jnp.zeros_like(pos)
    for e in ends:
        start = jnp.where(pos >= e, jnp.maximum(start, e), start)
    return start


def silu_of_dot(q, k):
    s = lax.dot_general(q, k, (((1,), (1,)), ((), ())), preferred_element_type=jnp.float32)
    h = s * HALF_SCALE
    return h + h * jnp.tanh(h)


def add_units(ends, q_base, q_ref, units, acc_ref):
    def row_tile(t, _):
        rows = pl.ds(pl.multiple_of(t * TILE, TILE), TILE)
        first = q_base + t * TILE
        last = first + TILE - 1
        low, high = start_of(ends, first), start_of(ends, last)
        pos = first + lax.broadcasted_iota(jnp.int32, (TILE, 1), 0)
        start = start_of(ends, pos)
        for owner, unit in units:
            base = owner * ROWS
            some = (base <= last) & (base + ROWS - 1 >= low)
            whole = (base + ROWS - 1 <= first) & (base >= high)

            @pl.when(whole)
            def _():
                w = silu_of_dot(q_ref[rows, :], unit[:, :HD]).astype(jnp.bfloat16)
                acc_ref[rows, :] += jnp.dot(w, unit[:, HD:], preferred_element_type=jnp.float32)

            @pl.when(some & jnp.logical_not(whole))
            def _():
                for part in range(ROWS // TILE):
                    k_first = base + part * TILE
                    keys = slice(part * TILE, (part + 1) * TILE)

                    @pl.when((k_first <= last) & (k_first + TILE - 1 >= low))
                    def _():
                        key = k_first + lax.broadcasted_iota(jnp.int32, (TILE, TILE), 1)
                        seen = (key <= pos) & (key >= start)
                        w = silu_of_dot(q_ref[rows, :], unit[keys, :HD])
                        w = jnp.where(seen, w, 0.0).astype(jnp.bfloat16)
                        acc_ref[rows, :] += jnp.dot(
                            w, unit[keys, HD:], preferred_element_type=jnp.float32
                        )

        return 0

    lax.fori_loop(0, ROWS // TILE, row_tile, 0)


def attend_kernel(names, first, hist_ref, q_ref, *refs):
    units, refs = refs[: len(names)], refs[len(names) :]
    acc_ref = refs[-1]
    if first:
        acc_ref[...] = jnp.zeros_like(acc_ref)
    else:
        acc_ref[...] = refs[0][...]
    me = lax.axis_index("ctx")
    ends = history_ends(hist_ref)
    owners = [unit_owner(*name) for name in names]
    add_units(ends, me * ROWS, q_ref, list(zip(owners, units)), acc_ref)


def estimate(units, weight=WEIGHT):
    return pl.CostEstimate(
        flops=weight * 4 * ROWS * ROWS * HD * units,
        bytes_accessed=1 << 20,
        transcendentals=ROWS * ROWS * units,
    )


def attend(hist, q, units, names, acc=None, weight=WEIGHT):
    first = acc is None
    return pl.pallas_call(
        functools.partial(attend_kernel, names, first),
        out_shape=jax.ShapeDtypeStruct((ROWS, HD), jnp.float32),
        in_specs=[SMEM] + [VMEM] * (1 + len(units) + (0 if first else 1)),
        out_specs=VMEM,
        cost_estimate=estimate(len(units), weight),
        compiler_params=params(),
    )(hist, q, *units, *(() if first else (acc,)))


def lent_kernel(names, first, final, hist_ref, q_ref, *refs):
    units, refs = refs[: len(names)], refs[len(names) :]
    acc_ref = refs[-1]
    if first:
        acc_ref[...] = jnp.zeros_like(acc_ref)
    else:
        acc_ref[...] = refs[0][...]
    me = lax.axis_index("ctx")

    @pl.when(me < PLANE)
    def _():
        ends = history_ends(hist_ref)
        owners = [unit_owner(*name) for name in names]
        add_units(ends, (me + PLANE) * ROWS, q_ref, list(zip(owners, units)), acc_ref)

    if final:
        refs[-2][...] = acc_ref[...].astype(jnp.bfloat16)


def attend_lent(hist, q, units, names, acc=None, final=False):
    first = acc is None
    return pl.pallas_call(
        functools.partial(lent_kernel, names, first, final),
        out_shape=jax.ShapeDtypeStruct((ROWS, HD), jnp.bfloat16 if final else jnp.float32),
        in_specs=[SMEM] + [VMEM] * (1 + len(units) + (0 if first else 1)),
        out_specs=VMEM,
        scratch_shapes=[pltpu.VMEM((ROWS, HD), jnp.float32)] if final else [],
        cost_estimate=estimate(len(units)),
        compiler_params=params(),
    )(hist, q, *units, *(() if first else (acc,)))


def last_kernel(names, hist_ref, q_ref, *refs):
    units = refs[: len(names)]
    acc_in, lent_ref, update_ref, out_ref, acc_ref = refs[len(names) :]
    me = lax.axis_index("ctx")
    acc_ref[...] = acc_in[...]

    @pl.when(me >= PLANE)
    def _():
        acc_ref[...] += lent_ref[...].astype(jnp.float32)

    ends = history_ends(hist_ref)
    owners = [unit_owner(*name) for name in names]
    add_units(ends, me * ROWS, q_ref, list(zip(owners, units)), acc_ref)
    a = acc_ref[...]
    mean = jnp.mean(a * a, axis=-1, keepdims=True)
    normed = a * lax.rsqrt(mean + 1e-6)
    out_ref[...] = (normed * update_ref[...].astype(jnp.float32)).astype(jnp.bfloat16)


def attend_last(hist, q, units, names, acc, lent, update):
    return pl.pallas_call(
        functools.partial(last_kernel, names),
        out_shape=jax.ShapeDtypeStruct((ROWS, HD), jnp.bfloat16),
        in_specs=[SMEM] + [VMEM] * (4 + len(units)),
        out_specs=VMEM,
        scratch_shapes=[pltpu.VMEM((ROWS, HD), jnp.float32)],
        cost_estimate=estimate(len(units)),
        compiler_params=params(),
    )(hist, q, *units, acc, lent, update)


def near_heads(head):
    chip, core = head // 2, head % 2
    even = chip + 1 - 2 * (chip % 2)
    odd = (chip + 3 + 2 * (chip % 2)) % 4
    return head, even * 2 + core, odd * 2 + core, (head + 4) % HEADS


def project_kernel(rows_ref, mine_ref, theirs_ref, out_ref):
    me = lax.axis_index("head")
    total = 0.0
    for head, w_ref in ((me, mine_ref), (me + 1 - 2 * (me % 2), theirs_ref)):
        rows = jnp.concatenate([rows_ref[h] for h in near_heads(head)], axis=1)
        total = total + jnp.dot(rows, w_ref[...], preferred_element_type=jnp.float32)
    mixed = total.astype(jnp.bfloat16)
    for h in range(HEADS):
        out_ref[h] = mixed[:, h * HD : (h + 1) * HD]


def project(rows, mine, theirs):
    return pl.pallas_call(
        project_kernel,
        out_shape=jax.ShapeDtypeStruct((HEADS, CHUNK, HD), jnp.bfloat16),
        in_specs=[VMEM] * 3,
        out_specs=VMEM,
        compiler_params=params(),
    )(rows, mine, theirs)


CORE = [(h, h ^ 1) for h in range(HEADS)]
X_EVEN = [(h, near_heads(h)[1]) for h in range(HEADS)]
X_FAR = [(h, near_heads(h)[3]) for h in range(HEADS)]
X_ODD = [(h, near_heads(h)[2]) for h in range(HEADS)]
UP = [(i, i + 1) for i in range(CTXS - 1)]
DOWN = [(i, i // PLANE * PLANE + (i - 1) % PLANE) for i in range(CTXS)]
LEND = [(i + PLANE, i) for i in range(PLANE)]
RETURN = [(i, i + PLANE) for i in range(PLANE)]


def gather_near(w):
    return [lax.ppermute(w, "head", perm) for perm in (X_EVEN, X_ODD, X_FAR)]


def body(ingest, src_shard, src_slot, hist_len, w_out):
    ingested, shards, slots = ingest[0, 0], src_shard[0], src_slot[0]
    move = functools.partial(lax.ppermute, axis_name="ctx")

    def to_all(x):
        return lax.all_to_all(x, "head", 0, 0, tiled=True)

    def to_owners(x):
        return lax.all_to_all(x, "batch", split_axis=0, concat_axis=0, tiled=True)

    unit_blocks, row_blocks = pick(shards, slots, ingested)
    w_late, unit_blocks = lax.optimization_barrier((w_out, unit_blocks))
    *near, row_blocks = lax.optimization_barrier((*gather_near(w_late), row_blocks))
    own = order_unit(shards, to_owners(unit_blocks))
    mine = jnp.concatenate([w_late, *near])
    theirs = lax.ppermute(mine, "head", CORE)
    row_blocks = to_owners(row_blocks)
    up, down = [own], [own]
    for step in range(4):
        up.append(move(up[-1], perm=UP))
        if step < 3:
            down.append(move(down[-1], perm=DOWN))
    q, update = order_rows(shards, row_blocks, (up[2], down[2]))
    lent_q = move(q, perm=LEND)
    acc = attend(
        hist_len, q, (own, up[1], down[1]), (("up", 0), ("up", 1), ("down", 1)), None, 1
    )
    lent = attend_lent(hist_len, lent_q, (own, down[1]), (("down", 0), ("down", 1)))
    acc = attend(hist_len, q, (up[2], down[2]), (("up", 2), ("down", 2)), acc, 2)
    lent = attend_lent(
        hist_len, lent_q, (down[2], down[3]), (("down", 2), ("down", 3)), lent, final=True
    )
    lent = move(lent, perm=RETURN)
    acc = attend(hist_len, q, (up[3], down[3]), (("up", 3), ("down", 3)), acc)
    gated = attend_last(hist_len, q, (up[4],), (("up", 4),), acc, lent, update)
    rows = to_all(gated.reshape(HEADS, CHUNK, HD))
    mixed = to_all(project(rows, mine, theirs))
    return mixed.reshape(1, ROWS, HD)


def solution(mesh):
    in_specs = (
        P("ctx", "batch", None, None, None, "head"),
        P("ctx", None, None),
        P("ctx", None, None),
        P("batch", None),
        P("head", None),
    )
    out_specs = P("batch", "ctx", "head")
    return jax.shard_map(body, mesh=mesh, in_specs=in_specs, out_specs=out_specs, check_vma=False)
```

```python
import functools
import math

import jax
import jax.numpy as jnp
from jax import lax
from jax.experimental import pallas as pl
from jax.experimental.pallas import tpu as pltpu
from jax.sharding import PartitionSpec as P

HD = 128
BLOCK = 128
PER_OWNER = 6
CAPACITY = 3
GROUPS = 4
CTXS = 16
PLANE = 8
HEADS = 8
ROWS = BLOCK * PER_OWNER
CHUNK = ROWS // HEADS
TILE = 256
WEIGHT = 8
HALF_SCALE = 0.5 / math.sqrt(HD)
VMEM = pl.BlockSpec(memory_space=pltpu.VMEM)
SMEM = pl.BlockSpec(memory_space=pltpu.SMEM)
ANY = pl.BlockSpec(memory_space=pl.ANY)


def params(mib=16):
    return pltpu.CompilerParams(vmem_limit_bytes=mib * 1024 * 1024)


def pick_kernel(shard_ref, slot_ref, ingest_ref, unit_ref, row_ref, buf, sems):
    me = lax.axis_index("batch")
    copies = []
    for g in range(GROUPS):
        seen = jnp.int32(0)
        slots = [jnp.int32(0)] * CAPACITY
        for k in range(PER_OWNER):
            hit = shard_ref[g, k] == me
            slot = slot_ref[g, k]
            for r in range(CAPACITY):
                slots[r] = jnp.where(hit & (seen == r), slot, slots[r])
            seen = seen + hit.astype(jnp.int32)
        for r in range(CAPACITY):
            at = g * CAPACITY + r
            copy = pltpu.make_async_copy(ingest_ref.at[slots[r]], buf.at[at], sems.at[at])
            copy.start()
            copies.append(copy)
    for at, copy in enumerate(copies):
        copy.wait()
        flat = buf[at].reshape(BLOCK, 4 * HD)
        unit_ref[at] = flat[:, HD : 3 * HD]
        row_ref[at, :, :HD] = flat[:, :HD]
        row_ref[at, :, HD:] = flat[:, 3 * HD :]


def pick(shards, slots, ingested):
    count = GROUPS * CAPACITY
    return pl.pallas_call(
        pick_kernel,
        out_shape=[jax.ShapeDtypeStruct((count, BLOCK, 2 * HD), jnp.bfloat16)] * 2,
        in_specs=[SMEM, SMEM, ANY],
        out_specs=[VMEM] * 2,
        scratch_shapes=[
            pltpu.VMEM((count, BLOCK, 4, HD), jnp.bfloat16),
            pltpu.SemaphoreType.DMA((count,)),
        ],
        compiler_params=params(56),
    )(shards, slots, ingested)


def block_places(shard_ref):
    me = lax.axis_index("batch")
    shards = [shard_ref[me, k] for k in range(PER_OWNER)]
    for k in range(PER_OWNER):
        rank = jnp.int32(0)
        for earlier in range(k):
            rank = rank + (shards[earlier] == shards[k]).astype(jnp.int32)
        yield slice(k * BLOCK, (k + 1) * BLOCK), shards[k] * CAPACITY + rank


def order_unit_kernel(shard_ref, in_ref, unit_ref):
    for rows, at in block_places(shard_ref):
        unit_ref[rows, :] = in_ref[at]


def order_unit(shards, blocks):
    return pl.pallas_call(
        order_unit_kernel,
        out_shape=jax.ShapeDtypeStruct((ROWS, 2 * HD), jnp.bfloat16),
        in_specs=[SMEM, VMEM],
        out_specs=VMEM,
        compiler_params=params(),
    )(shards, blocks)


def order_rows_kernel(shard_ref, in_ref, *refs):
    query_ref, update_ref = refs[-2:]
    for rows, at in block_places(shard_ref):
        query_ref[rows, :] = in_ref[at, :, :HD]
        update_ref[rows, :] = in_ref[at, :, HD:]


def order_rows(shards, blocks, earlier):
    return pl.pallas_call(
        order_rows_kernel,
        out_shape=[jax.ShapeDtypeStruct((ROWS, HD), jnp.bfloat16)] * 2,
        in_specs=[SMEM, VMEM] + [ANY] * len(earlier),
        out_specs=[VMEM] * 2,
        compiler_params=params(),
    )(shards, blocks, *earlier)


def unit_owner(stream, step):
    me = lax.axis_index("ctx")
    if step == 4:
        return me - step
    ahead = step if stream == "down" else PLANE - step
    return me // PLANE * PLANE + (me % PLANE + ahead) % PLANE


def history_ends(hist_ref):
    ends, total = [], jnp.int32(0)
    for u in range(4):
        total = total + hist_ref[0, u]
        ends.append(total)
    return ends


def start_of(ends, pos):
    start = jnp.zeros_like(pos)
    for e in ends:
        start = jnp.where(pos >= e, jnp.maximum(start, e), start)
    return start


def silu_of_dot(q, k):
    s = lax.dot_general(q, k, (((1,), (1,)), ((), ())), preferred_element_type=jnp.float32)
    h = s * HALF_SCALE
    return h + h * jnp.tanh(h)


def add_units(ends, q_base, q_ref, units, acc_ref):
    def row_tile(t, _):
        rows = pl.ds(pl.multiple_of(t * TILE, TILE), TILE)
        first = q_base + t * TILE
        last = first + TILE - 1
        low, high = start_of(ends, first), start_of(ends, last)
        pos = first + lax.broadcasted_iota(jnp.int32, (TILE, 1), 0)
        start = start_of(ends, pos)
        for owner, unit in units:
            base = owner * ROWS
            some = (base <= last) & (base + ROWS - 1 >= low)
            whole = (base + ROWS - 1 <= first) & (base >= high)

            @pl.when(whole)
            def _():
                w = silu_of_dot(q_ref[rows, :], unit[:, :HD]).astype(jnp.bfloat16)
                acc_ref[rows, :] += jnp.dot(w, unit[:, HD:], preferred_element_type=jnp.float32)

            @pl.when(some & jnp.logical_not(whole))
            def _():
                for part in range(ROWS // TILE):
                    k_first = base + part * TILE
                    keys = slice(part * TILE, (part + 1) * TILE)

                    @pl.when((k_first <= last) & (k_first + TILE - 1 >= low))
                    def _():
                        key = k_first + lax.broadcasted_iota(jnp.int32, (TILE, TILE), 1)
                        seen = (key <= pos) & (key >= start)
                        w = silu_of_dot(q_ref[rows, :], unit[keys, :HD])
                        w = jnp.where(seen, w, 0.0).astype(jnp.bfloat16)
                        acc_ref[rows, :] += jnp.dot(
                            w, unit[keys, HD:], preferred_element_type=jnp.float32
                        )

        return 0

    lax.fori_loop(0, ROWS // TILE, row_tile, 0)


def attend_kernel(names, first, hist_ref, q_ref, *refs):
    units, refs = refs[: len(names)], refs[len(names) :]
    acc_ref = refs[-1]
    if first:
        acc_ref[...] = jnp.zeros_like(acc_ref)
    else:
        acc_ref[...] = refs[0][...]
    me = lax.axis_index("ctx")
    ends = history_ends(hist_ref)
    owners = [unit_owner(*name) for name in names]
    add_units(ends, me * ROWS, q_ref, list(zip(owners, units)), acc_ref)


def estimate(units, weight=WEIGHT):
    return pl.CostEstimate(
        flops=weight * 4 * ROWS * ROWS * HD * units,
        bytes_accessed=1 << 20,
        transcendentals=ROWS * ROWS * units,
    )


def attend(hist, q, units, names, acc=None, weight=WEIGHT):
    first = acc is None
    return pl.pallas_call(
        functools.partial(attend_kernel, names, first),
        out_shape=jax.ShapeDtypeStruct((ROWS, HD), jnp.float32),
        in_specs=[SMEM] + [VMEM] * (1 + len(units) + (0 if first else 1)),
        out_specs=VMEM,
        cost_estimate=estimate(len(units), weight),
        compiler_params=params(),
    )(hist, q, *units, *(() if first else (acc,)))


def lent_kernel(names, first, final, hist_ref, q_ref, *refs):
    units, refs = refs[: len(names)], refs[len(names) :]
    acc_ref = refs[-1]
    if first:
        acc_ref[...] = jnp.zeros_like(acc_ref)
    else:
        acc_ref[...] = refs[0][...]
    me = lax.axis_index("ctx")

    @pl.when(me < PLANE)
    def _():
        ends = history_ends(hist_ref)
        owners = [unit_owner(*name) for name in names]
        add_units(ends, (me + PLANE) * ROWS, q_ref, list(zip(owners, units)), acc_ref)

    if final:
        refs[-2][...] = acc_ref[...].astype(jnp.bfloat16)


def attend_lent(hist, q, units, names, acc=None, final=False):
    first = acc is None
    return pl.pallas_call(
        functools.partial(lent_kernel, names, first, final),
        out_shape=jax.ShapeDtypeStruct((ROWS, HD), jnp.bfloat16 if final else jnp.float32),
        in_specs=[SMEM] + [VMEM] * (1 + len(units) + (0 if first else 1)),
        out_specs=VMEM,
        scratch_shapes=[pltpu.VMEM((ROWS, HD), jnp.float32)] if final else [],
        cost_estimate=estimate(len(units)),
        compiler_params=params(),
    )(hist, q, *units, *(() if first else (acc,)))


def last_kernel(names, hist_ref, q_ref, *refs):
    units = refs[: len(names)]
    acc_in, lent_ref, update_ref, out_ref, acc_ref = refs[len(names) :]
    me = lax.axis_index("ctx")
    acc_ref[...] = acc_in[...]

    @pl.when(me >= PLANE)
    def _():
        acc_ref[...] += lent_ref[...].astype(jnp.float32)

    ends = history_ends(hist_ref)
    owners = [unit_owner(*name) for name in names]
    add_units(ends, me * ROWS, q_ref, list(zip(owners, units)), acc_ref)
    a = acc_ref[...]
    mean = jnp.mean(a * a, axis=-1, keepdims=True)
    normed = a * lax.rsqrt(mean + 1e-6)
    out_ref[...] = (normed * update_ref[...].astype(jnp.float32)).astype(jnp.bfloat16)


def attend_last(hist, q, units, names, acc, lent, update):
    return pl.pallas_call(
        functools.partial(last_kernel, names),
        out_shape=jax.ShapeDtypeStruct((ROWS, HD), jnp.bfloat16),
        in_specs=[SMEM] + [VMEM] * (4 + len(units)),
        out_specs=VMEM,
        scratch_shapes=[pltpu.VMEM((ROWS, HD), jnp.float32)],
        cost_estimate=estimate(len(units)),
        compiler_params=params(),
    )(hist, q, *units, acc, lent, update)


def near_heads(head):
    chip, core = head // 2, head % 2
    even = chip + 1 - 2 * (chip % 2)
    odd = (chip + 3 + 2 * (chip % 2)) % 4
    return head, even * 2 + core, odd * 2 + core, (head + 4) % HEADS


def project_kernel(rows_ref, mine_ref, theirs_ref, out_ref):
    me = lax.axis_index("head")
    total = 0.0
    for head, w_ref in ((me, mine_ref), (me + 1 - 2 * (me % 2), theirs_ref)):
        rows = jnp.concatenate([rows_ref[h] for h in near_heads(head)], axis=1)
        total = total + jnp.dot(rows, w_ref[...], preferred_element_type=jnp.float32)
    mixed = total.astype(jnp.bfloat16)
    for h in range(HEADS):
        out_ref[h] = mixed[:, h * HD : (h + 1) * HD]


def project(rows, mine, theirs):
    return pl.pallas_call(
        project_kernel,
        out_shape=jax.ShapeDtypeStruct((HEADS, CHUNK, HD), jnp.bfloat16),
        in_specs=[VMEM] * 3,
        out_specs=VMEM,
        compiler_params=params(),
    )(rows, mine, theirs)


CORE = [(h, h ^ 1) for h in range(HEADS)]
X_EVEN = [(h, near_heads(h)[1]) for h in range(HEADS)]
X_FAR = [(h, near_heads(h)[3]) for h in range(HEADS)]
X_ODD = [(h, near_heads(h)[2]) for h in range(HEADS)]
UP = [(i, i // PLANE * PLANE + (i + 1) % PLANE) for i in range(CTXS)]
DOWN = [(j, i) for i, j in UP]
LAST_UP = [(i % PLANE if j % PLANE < 4 else i, j) for i, j in UP if j >= 4]
LEND = [(i + PLANE, i) for i in range(PLANE)]
RETURN = [(i, i + PLANE) for i in range(PLANE)]


def gather_near(w):
    return [lax.ppermute(w, "head", perm) for perm in (X_EVEN, X_ODD, X_FAR)]


def body(ingest, src_shard, src_slot, hist_len, w_out):
    ingested, shards, slots = ingest[0, 0], src_shard[0], src_slot[0]
    move = functools.partial(lax.ppermute, axis_name="ctx")

    def to_all(x):
        return lax.all_to_all(x, "head", 0, 0, tiled=True)

    def to_owners(x):
        return lax.all_to_all(x, "batch", split_axis=0, concat_axis=0, tiled=True)

    unit_blocks, row_blocks = pick(shards, slots, ingested)
    w_late, unit_blocks = lax.optimization_barrier((w_out, unit_blocks))
    *near, row_blocks = lax.optimization_barrier((*gather_near(w_late), row_blocks))
    own = order_unit(shards, to_owners(unit_blocks))
    mine = jnp.concatenate([w_late, *near])
    theirs = lax.ppermute(mine, "head", CORE)
    row_blocks = to_owners(row_blocks)
    up, down = [own], [own]
    for step in range(3):
        up.append(move(up[-1], perm=UP))
        down.append(move(down[-1], perm=DOWN))
    up.append(move(up[-1], perm=LAST_UP))
    names = [(("up", step), ("down", step)) for step in range(4)]
    units = list(zip(up, down))
    q, update = order_rows(shards, row_blocks, units[2])
    lent_q = move(q, perm=LEND)
    early, early_names = (own, *units[1]), (("up", 0), *names[1])
    acc = attend(hist_len, q, early, early_names, None, 1)
    lent = attend_lent(hist_len, lent_q, early, early_names)
    acc = attend(hist_len, q, units[2], names[2], acc, 2)
    lent = attend_lent(hist_len, lent_q, units[2], names[2], lent)
    lent = attend_lent(hist_len, lent_q, units[3], names[3], lent, final=True)
    lent = move(lent, perm=RETURN)
    acc = attend(hist_len, q, units[3], names[3], acc)
    gated = attend_last(hist_len, q, (up[4],), (("up", 4),), acc, lent, update)
    rows = to_all(gated.reshape(HEADS, CHUNK, HD))
    mixed = to_all(project(rows, mine, theirs))
    return mixed.reshape(1, ROWS, HD)


def solution(mesh):
    in_specs = (
        P("ctx", "batch", None, None, None, "head"),
        P("ctx", None, None),
        P("ctx", None, None),
        P("batch", None),
        P("head", None),
    )
    out_specs = P("batch", "ctx", "head")
    return jax.shard_map(body, mesh=mesh, in_specs=in_specs, out_specs=out_specs, check_vma=False)
```

```python
import functools
import math

import jax
import jax.numpy as jnp
from jax import lax
from jax.experimental import pallas as pl
from jax.experimental.pallas import tpu as pltpu
from jax.sharding import PartitionSpec as P

HD = 128
BLOCK = 128
PER_OWNER = 6
CAPACITY = 3
GROUPS = 4
CTXS = 16
PLANE = 8
HEADS = 8
ROWS = BLOCK * PER_OWNER
CHUNK = ROWS // HEADS
TILE = 256
WEIGHT = 2
HALF_SCALE = 0.5 / math.sqrt(HD)
VMEM = pl.BlockSpec(memory_space=pltpu.VMEM)
SMEM = pl.BlockSpec(memory_space=pltpu.SMEM)
ANY = pl.BlockSpec(memory_space=pl.ANY)


def params(mib=16):
    return pltpu.CompilerParams(vmem_limit_bytes=mib * 1024 * 1024)


def pick_kernel(shard_ref, slot_ref, ingest_ref, out_ref, buf, sems):
    me = lax.axis_index("batch")
    copies = []
    for g in range(GROUPS):
        seen = jnp.int32(0)
        slots = [jnp.int32(0)] * CAPACITY
        for k in range(PER_OWNER):
            hit = shard_ref[g, k] == me
            slot = slot_ref[g, k]
            for r in range(CAPACITY):
                slots[r] = jnp.where(hit & (seen == r), slot, slots[r])
            seen = seen + hit.astype(jnp.int32)
        for r in range(CAPACITY):
            at = g * CAPACITY + r
            copy = pltpu.make_async_copy(ingest_ref.at[slots[r]], buf.at[at], sems.at[at])
            copy.start()
            copies.append(copy)
    for at, copy in enumerate(copies):
        copy.wait()
        out_ref[at] = buf[at].reshape(BLOCK, 4 * HD)


def pick(shards, slots, ingested):
    count = GROUPS * CAPACITY
    return pl.pallas_call(
        pick_kernel,
        out_shape=jax.ShapeDtypeStruct((count, BLOCK, 4 * HD), jnp.bfloat16),
        in_specs=[SMEM, SMEM, ANY],
        out_specs=VMEM,
        scratch_shapes=[
            pltpu.VMEM((count, BLOCK, 4, HD), jnp.bfloat16),
            pltpu.SemaphoreType.DMA((count,)),
        ],
        compiler_params=params(56),
    )(shards, slots, ingested)


def block_places(shard_ref):
    me = lax.axis_index("batch")
    shards = [shard_ref[me, k] for k in range(PER_OWNER)]
    for k in range(PER_OWNER):
        rank = jnp.int32(0)
        for earlier in range(k):
            rank = rank + (shards[earlier] == shards[k]).astype(jnp.int32)
        yield slice(k * BLOCK, (k + 1) * BLOCK), shards[k] * CAPACITY + rank


def order_kernel(shard_ref, in_ref, unit_ref, query_ref, update_ref):
    for rows, at in block_places(shard_ref):
        query_ref[rows, :] = in_ref[at, :, :HD]
        unit_ref[rows, :] = in_ref[at, :, HD : 3 * HD]
        update_ref[rows, :] = in_ref[at, :, 3 * HD :]


def in_order(shards, blocks):
    shape = jax.ShapeDtypeStruct((ROWS, HD), jnp.bfloat16)
    return pl.pallas_call(
        order_kernel,
        out_shape=[jax.ShapeDtypeStruct((ROWS, 2 * HD), jnp.bfloat16), shape, shape],
        in_specs=[SMEM, VMEM],
        out_specs=[VMEM] * 3,
        compiler_params=params(),
    )(shards, blocks)


def unit_owner(stream, step):
    me = lax.axis_index("ctx")
    if stream == "up":
        return me - step
    return me // PLANE * PLANE + (me % PLANE + step) % PLANE


def history_ends(hist_ref):
    ends, total = [], jnp.int32(0)
    for u in range(4):
        total = total + hist_ref[0, u]
        ends.append(total)
    return ends


def start_of(ends, pos):
    start = jnp.zeros_like(pos)
    for e in ends:
        start = jnp.where(pos >= e, jnp.maximum(start, e), start)
    return start


def silu_of_dot(q, k):
    s = lax.dot_general(q, k, (((1,), (1,)), ((), ())), preferred_element_type=jnp.float32)
    h = s * HALF_SCALE
    return h + h * jnp.tanh(h)


def add_units(ends, q_base, q_ref, units, acc_ref):
    def row_tile(t, _):
        rows = pl.ds(pl.multiple_of(t * TILE, TILE), TILE)
        first = q_base + t * TILE
        last = first + TILE - 1
        low, high = start_of(ends, first), start_of(ends, last)
        pos = first + lax.broadcasted_iota(jnp.int32, (TILE, 1), 0)
        start = start_of(ends, pos)
        for owner, unit in units:
            base = owner * ROWS
            some = (base <= last) & (base + ROWS - 1 >= low)
            whole = (base + ROWS - 1 <= first) & (base >= high)

            @pl.when(whole)
            def _():
                w = silu_of_dot(q_ref[rows, :], unit[:, :HD]).astype(jnp.bfloat16)
                acc_ref[rows, :] += jnp.dot(w, unit[:, HD:], preferred_element_type=jnp.float32)

            @pl.when(some & jnp.logical_not(whole))
            def _():
                for part in range(ROWS // TILE):
                    k_first = base + part * TILE
                    keys = slice(part * TILE, (part + 1) * TILE)

                    @pl.when((k_first <= last) & (k_first + TILE - 1 >= low))
                    def _():
                        key = k_first + lax.broadcasted_iota(jnp.int32, (TILE, TILE), 1)
                        seen = (key <= pos) & (key >= start)
                        w = silu_of_dot(q_ref[rows, :], unit[keys, :HD])
                        w = jnp.where(seen, w, 0.0).astype(jnp.bfloat16)
                        acc_ref[rows, :] += jnp.dot(
                            w, unit[keys, HD:], preferred_element_type=jnp.float32
                        )

        return 0

    lax.fori_loop(0, ROWS // TILE, row_tile, 0)


def attend_kernel(names, first, hist_ref, q_ref, *refs):
    units, refs = refs[: len(names)], refs[len(names) :]
    acc_ref = refs[-1]
    if first:
        acc_ref[...] = jnp.zeros_like(acc_ref)
    else:
        acc_ref[...] = refs[0][...]
    me = lax.axis_index("ctx")
    ends = history_ends(hist_ref)
    owners = [unit_owner(*name) for name in names]
    add_units(ends, me * ROWS, q_ref, list(zip(owners, units)), acc_ref)


def estimate(units):
    return pl.CostEstimate(
        flops=WEIGHT * 4 * ROWS * ROWS * HD * units,
        bytes_accessed=1 << 20,
        transcendentals=ROWS * ROWS * units,
    )


def attend(hist, q, units, names, acc=None):
    first = acc is None
    return pl.pallas_call(
        functools.partial(attend_kernel, names, first),
        out_shape=jax.ShapeDtypeStruct((ROWS, HD), jnp.float32),
        in_specs=[SMEM] + [VMEM] * (1 + len(units) + (0 if first else 1)),
        out_specs=VMEM,
        cost_estimate=estimate(len(units)),
        compiler_params=params(),
    )(hist, q, *units, *(() if first else (acc,)))


def lent_kernel(names, first, final, hist_ref, q_ref, *refs):
    units, refs = refs[: len(names)], refs[len(names) :]
    acc_ref = refs[-1]
    if first:
        acc_ref[...] = jnp.zeros_like(acc_ref)
    else:
        acc_ref[...] = refs[0][...]
    me = lax.axis_index("ctx")

    @pl.when(me < PLANE)
    def _():
        ends = history_ends(hist_ref)
        owners = [unit_owner(*name) for name in names]
        add_units(ends, (me + PLANE) * ROWS, q_ref, list(zip(owners, units)), acc_ref)

    if final:
        refs[-2][...] = acc_ref[...].astype(jnp.bfloat16)


def attend_lent(hist, q, units, names, acc=None, final=False):
    first = acc is None
    return pl.pallas_call(
        functools.partial(lent_kernel, names, first, final),
        out_shape=jax.ShapeDtypeStruct((ROWS, HD), jnp.bfloat16 if final else jnp.float32),
        in_specs=[SMEM] + [VMEM] * (1 + len(units) + (0 if first else 1)),
        out_specs=VMEM,
        scratch_shapes=[pltpu.VMEM((ROWS, HD), jnp.float32)] if final else [],
        cost_estimate=estimate(len(units)),
        compiler_params=params(),
    )(hist, q, *units, *(() if first else (acc,)))


def last_kernel(names, hist_ref, q_ref, *refs):
    units = refs[: len(names)]
    acc_in, lent_ref, update_ref, out_ref, acc_ref = refs[len(names) :]
    me = lax.axis_index("ctx")
    acc_ref[...] = acc_in[...]

    @pl.when(me >= PLANE)
    def _():
        acc_ref[...] += lent_ref[...].astype(jnp.float32)

    ends = history_ends(hist_ref)
    owners = [unit_owner(*name) for name in names]
    add_units(ends, me * ROWS, q_ref, list(zip(owners, units)), acc_ref)
    a = acc_ref[...]
    mean = jnp.mean(a * a, axis=-1, keepdims=True)
    normed = a * lax.rsqrt(mean + 1e-6)
    out_ref[...] = (normed * update_ref[...].astype(jnp.float32)).astype(jnp.bfloat16)


def attend_last(hist, q, units, names, acc, lent, update):
    return pl.pallas_call(
        functools.partial(last_kernel, names),
        out_shape=jax.ShapeDtypeStruct((ROWS, HD), jnp.bfloat16),
        in_specs=[SMEM] + [VMEM] * (4 + len(units)),
        out_specs=VMEM,
        scratch_shapes=[pltpu.VMEM((ROWS, HD), jnp.float32)],
        cost_estimate=estimate(len(units)),
        compiler_params=params(),
    )(hist, q, *units, acc, lent, update)


def near_heads(head):
    chip, core = head // 2, head % 2
    even = chip + 1 - 2 * (chip % 2)
    odd = (chip + 3 + 2 * (chip % 2)) % 4
    return head, even * 2 + core, odd * 2 + core, (head + 4) % HEADS


def project_kernel(rows_ref, mine_ref, theirs_ref, out_ref):
    me = lax.axis_index("head")
    total = 0.0
    for head, w_ref in ((me, mine_ref), (me + 1 - 2 * (me % 2), theirs_ref)):
        rows = jnp.concatenate([rows_ref[h] for h in near_heads(head)], axis=1)
        total = total + jnp.dot(rows, w_ref[...], preferred_element_type=jnp.float32)
    mixed = total.astype(jnp.bfloat16)
    for h in range(HEADS):
        out_ref[h] = mixed[:, h * HD : (h + 1) * HD]


def project(rows, mine, theirs):
    return pl.pallas_call(
        project_kernel,
        out_shape=jax.ShapeDtypeStruct((HEADS, CHUNK, HD), jnp.bfloat16),
        in_specs=[VMEM] * 3,
        out_specs=VMEM,
        compiler_params=params(),
    )(rows, mine, theirs)


CORE = [(h, h ^ 1) for h in range(HEADS)]
X_EVEN = [(h, near_heads(h)[1]) for h in range(HEADS)]
X_ODD = [(h, near_heads(h)[2]) for h in range(HEADS)]
UP = [(i, i + 1) for i in range(CTXS - 1)]
DOWN = [(i, i // PLANE * PLANE + (i - 1) % PLANE) for i in range(CTXS)]
LEND = [(i + PLANE, i) for i in range(PLANE)]
RETURN = [(i, i + PLANE) for i in range(PLANE)]


def gather_w(w):
    cross = functools.partial(lax.ppermute, axis_name="head")
    half = HD // 2
    even, odd = cross(w, perm=X_EVEN), cross(w, perm=X_ODD)
    far = [cross(odd[:half], perm=X_EVEN), cross(even[half:], perm=X_ODD)]
    mine = jnp.concatenate([w, even, odd, *far])
    return mine, cross(mine, perm=CORE)


def body(ingest, src_shard, src_slot, hist_len, w_out):
    ingested, shards, slots = ingest[0, 0], src_shard[0], src_slot[0]
    move = functools.partial(lax.ppermute, axis_name="ctx")

    def to_all(x):
        return lax.all_to_all(x, "head", 0, 0, tiled=True)

    blocks = pick(shards, slots, ingested)
    w_late, blocks = lax.optimization_barrier((w_out, blocks))
    arrived = lax.all_to_all(blocks, "batch", split_axis=0, concat_axis=0, tiled=True)
    mine, theirs = gather_w(w_late)
    mine, theirs, arrived = lax.optimization_barrier((mine, theirs, arrived))
    own, q, update = in_order(shards, arrived)
    up, down = [own], [own]
    for step in range(4):
        up.append(move(up[-1], perm=UP))
        if step < 3:
            down.append(move(down[-1], perm=DOWN))
    lent_q = move(q, perm=LEND)
    acc = attend(hist_len, q, (own,), (("up", 0),))
    acc = attend(hist_len, q, (up[1], down[1]), (("up", 1), ("down", 1)), acc)
    lent = attend_lent(hist_len, lent_q, (own, down[1]), (("down", 0), ("down", 1)))
    acc = attend(hist_len, q, (up[2], down[2]), (("up", 2), ("down", 2)), acc)
    lent = attend_lent(
        hist_len, lent_q, (down[2], down[3]), (("down", 2), ("down", 3)), lent, final=True
    )
    lent = move(lent, perm=RETURN)
    acc = attend(hist_len, q, (up[3], down[3]), (("up", 3), ("down", 3)), acc)
    gated = attend_last(hist_len, q, (up[4],), (("up", 4),), acc, lent, update)
    rows = to_all(gated.reshape(HEADS, CHUNK, HD))
    mixed = to_all(project(rows, mine, theirs))
    return mixed.reshape(1, ROWS, HD)


def solution(mesh):
    in_specs = (
        P("ctx", "batch", None, None, None, "head"),
        P("ctx", None, None),
        P("ctx", None, None),
        P("batch", None),
        P("head", None),
    )
    out_specs = P("batch", "ctx", "head")
    return jax.shard_map(body, mesh=mesh, in_specs=in_specs, out_specs=out_specs, check_vma=False)
```
